512 devices in a mesh: freq: 64 (over y, z_hi, core), chan: 8 (over z_lo, x).
Axes of the slice: x: 4, y: 8, z: 8 (z_hi: 4, z_lo: 2; z = z_hi * 2 + z_lo), core: 2. Of those that a mesh axis runs over, the one named last changes fastest.
Arguments:
- record: bfloat16 [64, 6144, 2048], P('freq', None, 'chan'), may hold values from -12 to 12
Outputs:
- cross: float32 [2, 64, 2048, 1024], P(None, 'freq', 'chan')
The draws below stay inside these ranges and needn't reach their ends.
All inputs are finite; a program needn't handle non-finite values.
Results may differ from the reference program's by a relative error of at most 0.0032.
Values sent between devices are 32-bit elements; how exact they have to be, the bound alone decides.
No kernel may reach another device: no remote copies, remote signals or barrier semaphores. Data moves between devices by JAX's collectives and lax.ppermute only.
A program may use at most 64 MiB of HBM per device.

```python
import math
import jax
import jax.numpy as jnp
from jax import lax

CH_DEV = 256
SAMPLES = 6144
NBIN = 64
NEIGH = 40
WINDOWS = 64
CHANNELS = 2048
BAND = 1024
N_CHAN = 8


def draw_record(key, part):
    key = jax.random.fold_in(key, 11)
    noise_key, gain_key = jax.random.split(key, 2)
    shape = (WINDOWS, SAMPLES, CHANNELS)
    noise = jax.random.normal(noise_key, shape, jnp.float32)
    log_gain = jax.random.uniform(gain_key, (WINDOWS, 1, CHANNELS), jnp.float32, math.log(0.3), math.log(3.0))
    values = jnp.exp(log_gain) * noise
    return jnp.clip(values, -12.0, 12.0).astype(jnp.bfloat16)


def setup_inputs(seed: int = 0) -> dict:
    streams_of = jax.random.split(jax.random.key(seed), 2)
    record = draw_record(jax.random.fold_in(streams_of[1], 71), 0)
    return dict(record=record)


def dft_table():
    samples_idx = jnp.arange(SAMPLES, dtype=jnp.int32)
    stride = SAMPLES // (2 * NBIN)
    bin_index = 1 + jnp.arange(NBIN, dtype=jnp.int32) * stride
    phase = bin_index[:, None] * samples_idx[None, :] % SAMPLES
    angle = 2.0 * math.pi / SAMPLES * phase.astype(jnp.float32)
    return jnp.concatenate([jnp.cos(angle), -jnp.sin(angle)], axis=0).astype(jnp.bfloat16)

def neighbour_matrix():
    rows = jnp.arange(NBIN, dtype=jnp.int32)[:, None]
    cols = jnp.arange(NBIN, dtype=jnp.int32)[None, :]
    inside = (cols - rows >= -(NEIGH // 2)) & (cols - rows < NEIGH - NEIGH // 2)
    weights = inside.astype(jnp.float32)
    return weights / lax.optimization_barrier(jnp.sum(weights, axis=1, keepdims=True))

def band_product(own_block, wide_block):
    highest = lax.Precision.HIGHEST
    product_real = jnp.einsum('wi,wj->ij', own_block[:, 0], wide_block[:, 0], precision=highest) + jnp.einsum('wi,wj->ij', own_block[:, 1], wide_block[:, 1], precision=highest)
    product_imag = jnp.einsum('wi,wj->ij', own_block[:, 1], wide_block[:, 0], precision=highest) - jnp.einsum('wi,wj->ij', own_block[:, 0], wide_block[:, 1], precision=highest)
    stacked = jnp.stack([product_real, product_imag]) / WINDOWS
    own_count = stacked.shape[1]
    row_length = stacked.shape[2]
    flattened = stacked.reshape(2, own_count * row_length)
    padded_flat = jnp.pad(flattened, ((0, 0), (0, own_count)))
    skewed = padded_flat.reshape(2, own_count, row_length + 1)
    return skewed[:, :, :BAND]

def bin_cross(white_bin):
    padded = jnp.pad(white_bin, ((0, 0), (0, 0), (0, BAND)))

    def one_block(start):
        own_block = lax.dynamic_slice_in_dim(white_bin, start, CH_DEV, 2)
        wide_block = lax.dynamic_slice_in_dim(padded, start, CH_DEV + BAND, 2)
        return band_product(own_block, wide_block)
    starts = jnp.arange(N_CHAN, dtype=jnp.int32) * CH_DEV
    blocks = lax.map(one_block, starts)
    return blocks.transpose(1, 0, 2, 3).reshape(2, CHANNELS, BAND)

def reference(record):
    table_bins = dft_table().astype(jnp.float32)
    scaling = 1.0 / math.sqrt(SAMPLES)

    def one_window(window):
        product = jnp.dot(table_bins, window.astype(jnp.float32), precision=lax.Precision.HIGHEST)
        return product * scaling
    spectra = lax.map(one_window, record)
    spectra = spectra.reshape(WINDOWS, 2, NBIN, CHANNELS)
    power_bins = 0.5 * (spectra[:, 0] * spectra[:, 0] + spectra[:, 1] * spectra[:, 1])
    smooth = jnp.einsum('kj,wjc->wkc', neighbour_matrix(), power_bins, precision=lax.Precision.HIGHEST)
    whitened = spectra * lax.rsqrt(smooth + 1e-06)[:, None]
    per_bin = lax.map(bin_cross, whitened.transpose(2, 0, 1, 3))
    return per_bin.transpose(1, 0, 2, 3)
```

```python
import functools
import math

import jax
import jax.numpy as jnp
from jax import lax
from jax.experimental import pallas as pl
from jax.experimental.pallas import tpu as pltpu
from jax.sharding import PartitionSpec as P

NBIN = 64
NEIGH = 40
CHUNKS = 6
ROWS = 64
LANES = 128
WIDE = 256


def neighbour_weights():
    row = lax.broadcasted_iota(jnp.int32, (NBIN, NBIN), 0)
    col = lax.broadcasted_iota(jnp.int32, (NBIN, NBIN), 1)
    below, above = NEIGH // 2, NEIGH - NEIGH // 2
    inside = (col - row >= -below) & (col - row < above)
    count = jnp.minimum(row + above, NBIN) - jnp.maximum(row - below, 0)
    return jnp.where(inside, 1.0 / count.astype(jnp.float32), 0.0)


def base_angles(samples):
    stride, period = samples // (2 * NBIN), 2 * NBIN
    k = lax.broadcasted_iota(jnp.int32, (NBIN, period), 0)
    s = lax.broadcasted_iota(jnp.int32, (NBIN, period), 1)
    phase = s + stride * ((k * s) & (period - 1))
    return 2.0 * math.pi / samples * phase.astype(jnp.float32)


def whiten_kernel(samples, record_ref, out_ref, buf_ref, table_ref, sems):
    chunk = samples // CHUNKS
    period = 2 * NBIN
    turns = samples // period

    def fetch(n):
        part = pl.ds(n * chunk, chunk)
        return pltpu.make_async_copy(record_ref.at[0, part], buf_ref.at[part], sems.at[n])

    for n in range(CHUNKS):
        fetch(n).start()
    angle = base_angles(samples)
    cos, sin = jnp.cos(angle), jnp.sin(angle)
    for m in range(turns):
        c, s = math.cos(2.0 * math.pi * m / turns), math.sin(2.0 * math.pi * m / turns)
        part = pl.ds(m * period, period)
        table_ref[:NBIN, part] = (c * cos - s * sin).astype(jnp.bfloat16)
        table_ref[NBIN:, part] = (-(s * cos + c * sin)).astype(jnp.bfloat16)
    total = None
    for n in range(CHUNKS):
        fetch(n).wait()
        part = pl.ds(n * chunk, chunk)
        term = jnp.dot(table_ref[:, part], buf_ref[part], preferred_element_type=jnp.float32)
        total = term if total is None else total + term
    scaling = 1.0 / math.sqrt(samples)
    re, im = total[:NBIN] * scaling, total[NBIN:] * scaling
    power = 0.5 * (re * re + im * im)
    smooth = jnp.dot(neighbour_weights(), power, precision=lax.Precision.HIGHEST,
                     preferred_element_type=jnp.float32)
    gain = lax.rsqrt(smooth + 1e-06)
    half = re.shape[1] // LANES
    for n in range(half):
        part = slice(n * LANES, (n + 1) * LANES)
        out_ref[:, n, :] = (re * gain)[:, part]
        out_ref[:, half + n, :] = (im * gain)[:, part]


def whitened_bins(record):
    _, samples, ch = record.shape
    return pl.pallas_call(
        functools.partial(whiten_kernel, samples),
        in_specs=[pl.BlockSpec(memory_space=pltpu.HBM)],
        out_specs=pl.BlockSpec(memory_space=pltpu.VMEM),
        out_shape=jax.ShapeDtypeStruct((NBIN, 2 * ch // LANES, LANES), jnp.float32),
        scratch_shapes=[
            pltpu.VMEM((samples, ch), jnp.bfloat16),
            pltpu.VMEM((2 * NBIN, samples), jnp.bfloat16),
            pltpu.SemaphoreType.DMA((CHUNKS,)),
        ],
        compiler_params=pltpu.CompilerParams(vmem_limit_bytes=52 * 1024 * 1024),
        name="whiten",
    )(record)


def split_terms(x):
    high = x.astype(jnp.bfloat16)
    return high, (x - high.astype(jnp.float32)).astype(jnp.bfloat16)


def real_imag(block_ref):
    half = block_ref.shape[1] // 2
    tiles = [block_ref[:, n, :] for n in range(2 * half)]
    return jnp.concatenate(tiles[:half], axis=1), jnp.concatenate(tiles[half:], axis=1)


def left_kernel(own_ref, left_ref):
    re, im = real_imag(own_ref)
    scale = 1.0 / own_ref.shape[0]
    re, im = (re * scale).T, (im * scale).T
    left = jnp.concatenate(
        [jnp.concatenate([re, im], axis=1), jnp.concatenate([im, -re], axis=1)], axis=0
    )
    high, low = split_terms(left)
    left_ref[...] = jnp.concatenate([high, low, high], axis=1)


def left_terms(own):
    windows, pieces, lanes = own.shape
    return pl.pallas_call(
        left_kernel,
        in_specs=[pl.BlockSpec(memory_space=pltpu.VMEM)],
        out_specs=pl.BlockSpec(memory_space=pltpu.VMEM),
        out_shape=jax.ShapeDtypeStruct((pieces * lanes, 6 * windows), jnp.bfloat16),
        compiler_params=pltpu.CompilerParams(vmem_limit_bytes=16 * 1024 * 1024),
        cost_estimate=pl.CostEstimate(flops=0, bytes_accessed=1 << 20, transcendentals=0),
        name="left",
    )(own)


def region_kernel(first, count, fresh, left_ref, *refs):
    blocks = refs[:count + 1]
    out_ref, wide_ref, prod_ref, band_ref, sems = refs[count + 1 if fresh else count + 2:]
    ch = wide_ref.shape[1]
    tiles = ch // LANES
    row = lax.broadcasted_iota(jnp.int32, (ROWS, LANES), 0)
    lane = lax.broadcasted_iota(jnp.int32, (ROWS, LANES), 1)
    copies = []
    for n in range(count + 1):
        re, im = real_imag(blocks[n])
        high, low = split_terms(jnp.concatenate([re, im], axis=0))
        wide_ref[...] = jnp.concatenate([high, high, low], axis=0)
        prod_ref[:, n * ch:(n + 1) * ch] = jnp.dot(
            left_ref[...], wide_ref[...], preferred_element_type=jnp.float32
        )
        if n == 0:
            continue
        here = pl.ds((n - 1) * ch, ch)
        there = pl.ds((first + n - 1) * ch, ch)
        for part in range(2):
            for start in range(0, ch, ROWS):
                low_rows = start % LANES
                head = (start // LANES) + (n - 1) * tiles
                source = (lane + row + low_rows) % LANES
                keep = lane < LANES - low_rows - row
                rows = pl.ds(part * ch + start, ROWS)

                def turned(v):
                    tile = prod_ref[rows, pl.ds((head + v) * LANES, LANES)]
                    return jnp.take_along_axis(tile, source, axis=1, mode="promise_in_bounds")

                before = turned(0)
                for v in range(tiles):
                    after = turned(v + 1)
                    band_ref[part, pl.ds(start, ROWS), pl.ds((n - 1) * ch + v * LANES, LANES)] = (
                        jnp.where(keep, before, after)
                    )
                    before = after
            copy = pltpu.make_async_copy(
                band_ref.at[part, :, here], out_ref.at[part, 0, :, there], sems.at[n - 1, part]
            )
            copy.start()
            copies.append(copy)
    for copy in copies:
        copy.wait()


def region(left, blocks, first, band, out=None):
    windows, pieces, lanes = blocks[0].shape
    ch = pieces * lanes // 2
    count = len(blocks) - 1
    vmem = pl.BlockSpec(memory_space=pltpu.VMEM)
    hbm = pl.BlockSpec(memory_space=pltpu.HBM)
    fresh = out is None
    return pl.pallas_call(
        functools.partial(region_kernel, first, count, fresh),
        in_specs=[vmem] * (count + 2) + ([] if fresh else [hbm]),
        out_specs=hbm,
        out_shape=jax.ShapeDtypeStruct((2, 1, ch, band), jnp.float32),
        scratch_shapes=[
            pltpu.VMEM((6 * windows, ch), jnp.bfloat16),
            pltpu.VMEM((2 * ch, (count + 1) * ch), jnp.float32),
            pltpu.VMEM((2, ch, count * ch), jnp.float32),
            pltpu.SemaphoreType.DMA((count, 2)),
        ],
        input_output_aliases={} if fresh else {count + 2: 0},
        compiler_params=pltpu.CompilerParams(vmem_limit_bytes=32 * 1024 * 1024),
        cost_estimate=pl.CostEstimate(flops=0, bytes_accessed=3 << 20, transcendentals=0),
        name="region",
    )(left, *blocks, *([] if fresh else [out]))


def cross_all(blocks):
    _, pieces, lanes = blocks[0].shape
    reach = len(blocks) - 1
    left = left_terms(blocks[0])
    band = reach * pieces * lanes // 2
    out = region(left, blocks[3:5], 3, band)
    out = region(left, blocks[0:2], 0, band, out)
    return region(left, blocks[1:4], 1, band, out)


def upper_blocks(own):
    count = lax.axis_size("chan")
    half = count // 2

    def moved(array, pairs):
        return lax.ppermute(array, "chan", pairs)

    fourth = moved(own, [(c, c - half) for c in range(half, count)])
    third = moved(own, [(c, c - 3) for c in range(3, count)])
    first = moved(own, [(c, c - 1) for c in range(1, count)])
    handed = jnp.where(lax.axis_index("chan") < 2, fourth, own)
    second = moved(
        handed,
        [(c, c - 2) for c in range(2, count) if c // half == (c - 2) // half]
        + [(c, c + 2) for c in range(2)],
    )
    return [first, second, third, fourth]


def shards(record):
    bins = whitened_bins(record)
    own = lax.all_to_all(bins, "freq", split_axis=0, concat_axis=0, tiled=True)
    return cross_all([own] + upper_blocks(own))


def solution(mesh):
    return jax.shard_map(
        shards,
        mesh=mesh,
        in_specs=(P("freq", None, "chan"),),
        out_specs=P(None, "freq", "chan", None),
        check_vma=False,
    )
```

```python
import functools
import math

import jax
import jax.numpy as jnp
from jax import lax
from jax.experimental import pallas as pl
from jax.experimental.pallas import tpu as pltpu
from jax.sharding import Mesh, PartitionSpec as P

NBIN = 64
NEIGH = 40
CHUNKS = 4
ROWS = 64
LANES = 128


def bin_of(row):
    return 2 * (row & (NBIN // 2 - 1)) + row // (NBIN // 2)


def neighbour_weights():
    row = bin_of(lax.broadcasted_iota(jnp.int32, (NBIN, NBIN), 0))
    col = bin_of(lax.broadcasted_iota(jnp.int32, (NBIN, NBIN), 1))
    below, above = NEIGH // 2, NEIGH - NEIGH // 2
    inside = (col - row >= -below) & (col - row < above)
    count = jnp.minimum(row + above, NBIN) - jnp.maximum(row - below, 0)
    return jnp.where(inside, 1.0 / count.astype(jnp.float32), 0.0)


def base_angles(samples):
    stride, period = samples // (2 * NBIN), 2 * NBIN
    k = bin_of(lax.broadcasted_iota(jnp.int32, (NBIN, period), 0))
    s = lax.broadcasted_iota(jnp.int32, (NBIN, period), 1)
    phase = s + stride * ((k * s) & (period - 1))
    return 2.0 * math.pi / samples * phase.astype(jnp.float32)


def whiten_kernel(samples, core_ref, record_ref, keep_ref, send_ref, buf_ref, table_ref, sems):
    chunk = samples // CHUNKS
    quarter = samples // 4
    period = 2 * NBIN
    turns = samples // period

    def fetch(n):
        part = pl.ds(n * chunk, chunk)
        return pltpu.make_async_copy(record_ref.at[0, part], buf_ref.at[part], sems.at[n])

    for n in range(CHUNKS):
        fetch(n).start(priority=n % 2)
    angle = base_angles(samples)
    cos, sin = jnp.cos(angle), jnp.sin(angle)
    for m in range(quarter // period):
        c, s = math.cos(2.0 * math.pi * m / turns), math.sin(2.0 * math.pi * m / turns)
        part = pl.ds(m * period, period)
        table_ref[:NBIN, part] = (c * cos - s * sin).astype(jnp.bfloat16)
        table_ref[NBIN:, part] = (-s * cos - c * sin).astype(jnp.bfloat16)
    sums = [None] * 4
    for n in range(CHUNKS):
        fetch(n).wait()
        q, start = divmod(n * chunk, quarter)
        term = jnp.dot(table_ref[:, pl.ds(start, chunk)], buf_ref[pl.ds(n * chunk, chunk)],
                       preferred_element_type=jnp.float32)
        sums[q] = term if sums[q] is None else sums[q] + term
    even, odd = sums[0] - sums[2], sums[1] - sums[3]
    scaling = 1.0 / math.sqrt(samples)
    re = (even[:NBIN] + odd[NBIN:]) * scaling
    im = (even[NBIN:] - odd[:NBIN]) * scaling
    power = 0.5 * (re * re + im * im)
    smooth = jnp.dot(neighbour_weights(), power, precision=lax.Precision.HIGHEST,
                     preferred_element_type=jnp.float32)
    gain = lax.rsqrt(smooth + 1e-06)
    re, im = re * gain, im * gain
    even_core = core_ref[0] == 0
    pieces = re.shape[1] // LANES
    for p, value in enumerate((re, im)):
        lower, upper = value[:NBIN // 2], value[NBIN // 2:]
        keep, send = jnp.where(even_core, lower, upper), jnp.where(even_core, upper, lower)
        for n in range(pieces):
            part = slice(n * LANES, (n + 1) * LANES)
            keep_ref[:, p * pieces + n, :] = keep[:, part]
            send_ref[:, p * pieces + n, :] = send[:, part]


def whitened_bins(core, record):
    _, samples, ch = record.shape
    vmem = pl.BlockSpec(memory_space=pltpu.VMEM)
    shape = jax.ShapeDtypeStruct((NBIN // 2, 2 * ch // LANES, LANES), jnp.float32)
    return pl.pallas_call(
        functools.partial(whiten_kernel, samples),
        in_specs=[
            pl.BlockSpec(memory_space=pltpu.SMEM),
            pl.BlockSpec(memory_space=pltpu.HBM),
        ],
        out_specs=(vmem, vmem),
        out_shape=(shape, shape),
        scratch_shapes=[
            pltpu.VMEM((samples, ch), jnp.bfloat16),
            pltpu.VMEM((2 * NBIN, samples // 4), jnp.bfloat16),
            pltpu.SemaphoreType.DMA((CHUNKS,)),
        ],
        compiler_params=pltpu.CompilerParams(vmem_limit_bytes=52 * 1024 * 1024),
        name="whiten",
    )(core, record)


def split_terms(x):
    high = x.astype(jnp.bfloat16)
    return high, (x - high.astype(jnp.float32)).astype(jnp.bfloat16)


def real_imag(block_ref):
    half = block_ref.shape[1] // 2
    tiles = [block_ref[:, n, :] for n in range(2 * half)]
    return jnp.concatenate(tiles[:half], axis=1), jnp.concatenate(tiles[half:], axis=1)


def product(left_ref, block_ref, wide_ref, out_ref):
    re, im = real_imag(block_ref)
    high, low = split_terms(jnp.concatenate([re, im], axis=0))
    wide_ref[...] = jnp.concatenate([high, high, low], axis=0)
    halves, parts, rows, ch = out_ref.shape
    for a in range(halves):
        here = pl.ds(a * parts * rows, parts * rows)
        out_ref[a] = jnp.dot(
            left_ref[here], wide_ref[...], preferred_element_type=jnp.float32
        ).reshape(parts, rows, ch)


def own_kernel(own_ref, left_ref, prod_ref, wide_ref):
    re, im = real_imag(own_ref)
    scale = 1.0 / own_ref.shape[0]
    re, im = (re * scale).T, (im * scale).T
    rows = re.shape[0] // 2
    for a in range(2):
        r, i = re[a * rows:(a + 1) * rows], im[a * rows:(a + 1) * rows]
        left = jnp.concatenate(
            [jnp.concatenate([r, i], axis=1), jnp.concatenate([i, -r], axis=1)], axis=0
        )
        high, low = split_terms(left)
        left_ref[2 * a * rows:2 * (a + 1) * rows] = jnp.concatenate([high, low, high], axis=1)
    product(left_ref, own_ref, wide_ref, prod_ref)


def product_shape(ch):
    return jax.ShapeDtypeStruct((2, 2, ch // 2, ch), jnp.float32)


def own_terms(own):
    windows, pieces, lanes = own.shape
    ch = pieces * lanes // 2
    vmem = pl.BlockSpec(memory_space=pltpu.VMEM)
    return pl.pallas_call(
        own_kernel,
        in_specs=[vmem],
        out_specs=(vmem, vmem),
        out_shape=(
            jax.ShapeDtypeStruct((2 * ch, 6 * windows), jnp.bfloat16),
            product_shape(ch),
        ),
        scratch_shapes=[pltpu.VMEM((6 * windows, ch), jnp.bfloat16)],
        compiler_params=pltpu.CompilerParams(vmem_limit_bytes=16 * 1024 * 1024),
        cost_estimate=pl.CostEstimate(flops=0, bytes_accessed=1 << 20, transcendentals=0),
        name="own",
    )(own)


def region_kernel(first, given, keep, fresh, left_ref, *refs):
    count = len(given)
    blocks, refs = refs[:count], refs[count if fresh else count + 1:]
    out_ref, kept, refs = refs[0], refs[1:1 + len(keep)], refs[1 + len(keep):]
    wide_ref, prod_ref, band_ref, sems = refs
    products = []
    for n in range(count):
        if given[n]:
            products.append(blocks[n])
            continue
        target = kept[keep.index(n)] if n in keep else prod_ref.at[n]
        product(left_ref, blocks[n], wide_ref, target)
        products.append(target)
    ch = wide_ref.shape[1]
    rows = ch // 2
    tiles = ch // LANES
    row = lax.broadcasted_iota(jnp.int32, (ROWS, LANES), 0)
    lane = lax.broadcasted_iota(jnp.int32, (ROWS, LANES), 1)
    copies = []
    for a in range(2):
        for part in range(2):
            for start in range(0, rows, ROWS):
                source = (lane + row + start) % LANES
                stays = lane < LANES - start - row

                def turned(tile):
                    n, lanes = divmod(tile, tiles)
                    value = products[n][a, part, pl.ds(start, ROWS), pl.ds(lanes * LANES, LANES)]
                    return jnp.take_along_axis(value, source, axis=1, mode="promise_in_bounds")

                before = turned(a)
                for v in range((count - 1) * tiles):
                    after = turned(a + v + 1)
                    band_ref[part, pl.ds(a * rows + start, ROWS), pl.ds(v * LANES, LANES)] = (
                        jnp.where(stays, before, after)
                    )
                    before = after
            here = pl.ds(a * rows, rows)
            there = pl.ds(first * ch, (count - 1) * ch)
            copy = pltpu.make_async_copy(
                band_ref.at[part, here], out_ref.at[part, 0, here, there], sems.at[a, part]
            )
            copy.start()
            copies.append(copy)
    for copy in copies:
        copy.wait()


def region(left, blocks, first, band, out=None, keep=()):
    ch = left.shape[0] // 2
    depth = left.shape[1]
    count = len(blocks)
    vmem = pl.BlockSpec(memory_space=pltpu.VMEM)
    hbm = pl.BlockSpec(memory_space=pltpu.HBM)
    fresh = out is None
    given = tuple(block.ndim == 4 for block in blocks)
    return pl.pallas_call(
        functools.partial(region_kernel, first, given, keep, fresh),
        in_specs=[vmem] * (count + 1) + ([] if fresh else [hbm]),
        out_specs=(hbm,) + (vmem,) * len(keep),
        out_shape=(jax.ShapeDtypeStruct((2, 1, ch, band), jnp.float32),)
        + (product_shape(ch),) * len(keep),
        scratch_shapes=[
            pltpu.VMEM((depth, ch), jnp.bfloat16),
            pltpu.VMEM((count,) + product_shape(ch).shape, jnp.float32),
            pltpu.VMEM((2, ch, (count - 1) * ch), jnp.float32),
            pltpu.SemaphoreType.DMA((2, 2)),
        ],
        input_output_aliases={} if fresh else {count + 1: 0},
        compiler_params=pltpu.CompilerParams(vmem_limit_bytes=24 * 1024 * 1024),
        cost_estimate=pl.CostEstimate(flops=0, bytes_accessed=3 << 20, transcendentals=0),
        name="region",
    )(left, *blocks, *([] if fresh else [out]))


def cross_all(blocks):
    own, first, second, third, fourth = blocks
    _, pieces, lanes = own.shape
    band = (len(blocks) - 1) * pieces * lanes // 2
    left, own_product = own_terms(own)
    out, third_product = region(left, [third, fourth], 3, band, keep=(0,))
    out, first_product = region(left, [own_product, first], 0, band, out, keep=(1,))
    out, = region(left, [first_product, second, third_product], 1, band, out)
    return out


def upper_blocks(own):
    chan = ("z", "x")
    count = lax.axis_size(chan)
    half = count // 2

    def moved(array, pairs):
        return lax.ppermute(array, chan, pairs)

    fourth = moved(own, [(c, c - half) for c in range(half, count)])
    third = moved(own, [(c, c - 3) for c in range(3, count)])
    first = moved(own, [(c, c - 1) for c in range(1, count)])
    handed = jnp.where(lax.axis_index(chan) < 2, fourth, own)
    second = moved(
        handed,
        [(c, c - 2) for c in range(2, count) if c // half == (c - 2) // half]
        + [(c, c + 2) for c in range(2)],
    )
    return [first, second, third, fourth]


def shards(record):
    core = lax.axis_index("core").astype(jnp.int32).reshape(1)
    keep, send = whitened_bins(core, record)
    got = lax.ppermute(send, "core", [(0, 1), (1, 0)])
    pairs = jnp.concatenate([keep, got], axis=1)
    own = lax.all_to_all(pairs, ("y", "zh"), split_axis=0, concat_axis=0, tiled=True)
    own = own.reshape(NBIN, keep.shape[1], LANES)
    return cross_all([own] + upper_blocks(own))


def solution(mesh):
    freq, chan = mesh.devices.shape
    devices = mesh.devices.reshape(8, freq // 16, 2, 2, chan // 2)
    fine = Mesh(devices, ("y", "zh", "core", "z", "x"))
    return jax.shard_map(
        shards,
        mesh=fine,
        in_specs=(P(("y", "zh", "core"), None, ("z", "x")),),
        out_specs=P(None, ("y", "zh", "core"), ("z", "x"), None),
        check_vma=False,
    )
```

```python
import functools
import math

import jax
import jax.numpy as jnp
from jax import lax
from jax.experimental import pallas as pl
from jax.experimental.pallas import tpu as pltpu
from jax.sharding import PartitionSpec as P

NBIN = 64
NEIGH = 40
CHUNKS = 6
ROWS = 64
LANES = 128


def split_terms(x, rest=jnp.bfloat16):
    high = x.astype(jnp.bfloat16)
    return high, (x - high.astype(jnp.float32)).astype(rest)


def smoothed(power):
    row = lax.broadcasted_iota(jnp.int32, (NBIN, NBIN), 0)
    col = lax.broadcasted_iota(jnp.int32, (NBIN, NBIN), 1)
    below, above = NEIGH // 2, NEIGH - NEIGH // 2
    inside = ((col - row >= -below) & (col - row < above)).astype(jnp.float32)
    inside = inside.astype(jnp.bfloat16)
    high, rest = split_terms(power, jnp.float32)
    middle, low = split_terms(rest, jnp.bfloat16)
    total = jnp.dot(
        jnp.concatenate([inside, inside, inside], axis=1),
        jnp.concatenate([high, middle, low], axis=0),
        preferred_element_type=jnp.float32,
    )
    first = lax.broadcasted_iota(jnp.int32, power.shape, 0)
    count = jnp.minimum(first + above, NBIN) - jnp.maximum(first - below, 0)
    return total / count.astype(jnp.float32)


def base_angles(samples):
    stride, period = samples // (2 * NBIN), 2 * NBIN
    k = lax.broadcasted_iota(jnp.int32, (NBIN, period), 0)
    s = lax.broadcasted_iota(jnp.int32, (NBIN, period), 1)
    phase = s + stride * ((k * s) & (period - 1))
    return 2.0 * math.pi / samples * phase.astype(jnp.float32)


def whiten_kernel(samples, record_ref, out_ref, buf_ref, table_ref, sems):
    chunk = samples // CHUNKS
    period = 2 * NBIN
    turns = samples // period

    def fetch(n):
        part = pl.ds(n * chunk, chunk)
        return pltpu.make_async_copy(record_ref.at[0, part], buf_ref.at[part], sems.at[n])

    for n in range(CHUNKS):
        fetch(n).start()
    angle = base_angles(samples)
    cos, sin = jnp.cos(angle), jnp.sin(angle)
    for m in range(turns):
        c, s = math.cos(2.0 * math.pi * m / turns), math.sin(2.0 * math.pi * m / turns)
        part = pl.ds(m * period, period)
        table_ref[:NBIN, part] = (c * cos - s * sin).astype(jnp.bfloat16)
        table_ref[NBIN:, part] = (-(s * cos + c * sin)).astype(jnp.bfloat16)
    total = None
    for n in range(CHUNKS):
        fetch(n).wait()
        part = pl.ds(n * chunk, chunk)
        term = jnp.dot(table_ref[:, part], buf_ref[part], preferred_element_type=jnp.float32)
        total = term if total is None else total + term
    scaling = 1.0 / math.sqrt(samples)
    re, im = total[:NBIN] * scaling, total[NBIN:] * scaling
    power = 0.5 * (re * re + im * im)
    gain = lax.rsqrt(smoothed(power) + 1e-06)
    half = re.shape[1] // LANES
    for n in range(half):
        part = slice(n * LANES, (n + 1) * LANES)
        out_ref[:, n, :] = (re * gain)[:, part]
        out_ref[:, half + n, :] = (im * gain)[:, part]


def whitened_bins(record):
    _, samples, ch = record.shape
    return pl.pallas_call(
        functools.partial(whiten_kernel, samples),
        in_specs=[pl.BlockSpec(memory_space=pltpu.HBM)],
        out_specs=pl.BlockSpec(memory_space=pltpu.VMEM),
        out_shape=jax.ShapeDtypeStruct((NBIN, 2 * ch // LANES, LANES), jnp.float32),
        scratch_shapes=[
            pltpu.VMEM((samples, ch), jnp.bfloat16),
            pltpu.VMEM((2 * NBIN, samples), jnp.bfloat16),
            pltpu.SemaphoreType.DMA((CHUNKS,)),
        ],
        compiler_params=pltpu.CompilerParams(vmem_limit_bytes=52 * 1024 * 1024),
        name="whiten",
    )(record)


def real_imag(block_ref):
    half = block_ref.shape[1] // 2
    tiles = [block_ref[:, n, :] for n in range(2 * half)]
    return jnp.concatenate(tiles[:half], axis=1), jnp.concatenate(tiles[half:], axis=1)


def product(left_ref, block_ref, wide_ref, out_ref):
    re, im = real_imag(block_ref)
    high, low = split_terms(jnp.concatenate([re, im], axis=0))
    wide_ref[...] = jnp.concatenate([high, high, low], axis=0)
    halves, parts, rows, ch = out_ref.shape
    for a in range(halves):
        here = pl.ds(a * parts * rows, parts * rows)
        out_ref[a] = jnp.dot(
            left_ref[here], wide_ref[...], preferred_element_type=jnp.float32
        ).reshape(parts, rows, ch)


def own_kernel(own_ref, left_ref, prod_ref, wide_ref):
    re, im = real_imag(own_ref)
    scale = 1.0 / own_ref.shape[0]
    re, im = (re * scale).T, (im * scale).T
    rows = re.shape[0] // 2
    for a in range(2):
        r, i = re[a * rows:(a + 1) * rows], im[a * rows:(a + 1) * rows]
        left = jnp.concatenate(
            [jnp.concatenate([r, i], axis=1), jnp.concatenate([i, -r], axis=1)], axis=0
        )
        high, low = split_terms(left)
        left_ref[2 * a * rows:2 * (a + 1) * rows] = jnp.concatenate([high, low, high], axis=1)
    product(left_ref, own_ref, wide_ref, prod_ref)


def product_shape(ch):
    return jax.ShapeDtypeStruct((2, 2, ch // 2, ch), jnp.float32)


def own_terms(own):
    windows, pieces, lanes = own.shape
    ch = pieces * lanes // 2
    vmem = pl.BlockSpec(memory_space=pltpu.VMEM)
    return pl.pallas_call(
        own_kernel,
        in_specs=[vmem],
        out_specs=(vmem, vmem),
        out_shape=(
            jax.ShapeDtypeStruct((2 * ch, 6 * windows), jnp.bfloat16),
            product_shape(ch),
        ),
        scratch_shapes=[pltpu.VMEM((6 * windows, ch), jnp.bfloat16)],
        compiler_params=pltpu.CompilerParams(vmem_limit_bytes=16 * 1024 * 1024),
        cost_estimate=pl.CostEstimate(flops=0, bytes_accessed=1 << 20, transcendentals=0),
        name="own",
    )(own)


def region_kernel(first, given, keep, fresh, left_ref, *refs):
    count = len(given)
    blocks, refs = refs[:count], refs[count if fresh else count + 1:]
    out_ref, kept, refs = refs[0], refs[1:1 + len(keep)], refs[1 + len(keep):]
    wide_ref, prod_ref, band_ref, sems = refs
    products = []
    for n in range(count):
        if given[n]:
            products.append(blocks[n])
            continue
        target = kept[keep.index(n)] if n in keep else prod_ref.at[n]
        product(left_ref, blocks[n], wide_ref, target)
        products.append(target)
    ch = wide_ref.shape[1]
    rows = ch // 2
    tiles = ch // LANES
    row = lax.broadcasted_iota(jnp.int32, (ROWS, LANES), 0)
    lane = lax.broadcasted_iota(jnp.int32, (ROWS, LANES), 1)
    copies = []
    for a in range(2):
        for part in range(2):
            for start in range(0, rows, ROWS):
                source = (lane + row + start) % LANES
                stays = lane < LANES - start - row

                def turned(tile):
                    n, lanes = divmod(tile, tiles)
                    value = products[n][a, part, pl.ds(start, ROWS), pl.ds(lanes * LANES, LANES)]
                    return jnp.take_along_axis(value, source, axis=1, mode="promise_in_bounds")

                before = turned(a)
                for v in range((count - 1) * tiles):
                    after = turned(a + v + 1)
                    band_ref[part, pl.ds(a * rows + start, ROWS), pl.ds(v * LANES, LANES)] = (
                        jnp.where(stays, before, after)
                    )
                    before = after
            here = pl.ds(a * rows, rows)
            there = pl.ds(first * ch, (count - 1) * ch)
            copy = pltpu.make_async_copy(
                band_ref.at[part, here], out_ref.at[part, 0, here, there], sems.at[a, part]
            )
            copy.start()
            copies.append(copy)
    for copy in copies:
        copy.wait()


def region(left, blocks, first, band, out=None, keep=()):
    ch = left.shape[0] // 2
    depth = left.shape[1]
    count = len(blocks)
    vmem = pl.BlockSpec(memory_space=pltpu.VMEM)
    hbm = pl.BlockSpec(memory_space=pltpu.HBM)
    fresh = out is None
    given = tuple(block.ndim == 4 for block in blocks)
    return pl.pallas_call(
        functools.partial(region_kernel, first, given, keep, fresh),
        in_specs=[vmem] * (count + 1) + ([] if fresh else [hbm]),
        out_specs=(hbm,) + (vmem,) * len(keep),
        out_shape=(jax.ShapeDtypeStruct((2, 1, ch, band), jnp.float32),)
        + (product_shape(ch),) * len(keep),
        scratch_shapes=[
            pltpu.VMEM((depth, ch), jnp.bfloat16),
            pltpu.VMEM((count,) + product_shape(ch).shape, jnp.float32),
            pltpu.VMEM((2, ch, (count - 1) * ch), jnp.float32),
            pltpu.SemaphoreType.DMA((2, 2)),
        ],
        input_output_aliases={} if fresh else {count + 1: 0},
        compiler_params=pltpu.CompilerParams(vmem_limit_bytes=24 * 1024 * 1024),
        cost_estimate=pl.CostEstimate(flops=0, bytes_accessed=3 << 20, transcendentals=0),
        name="region",
    )(left, *blocks, *([] if fresh else [out]))


def cross_all(blocks):
    own, first, second, third, fourth = blocks
    _, pieces, lanes = own.shape
    band = (len(blocks) - 1) * pieces * lanes // 2
    left, own_product = own_terms(own)
    out, third_product = region(left, [third, fourth], 3, band, keep=(0,))
    out, second_product = region(left, [second, third_product], 2, band, out, keep=(0,))
    out, = region(left, [own_product, first, second_product], 0, band, out)
    return out


def upper_block(own, offset):
    count = lax.axis_size("chan")
    return lax.ppermute(own, "chan", [(c, c - offset) for c in range(offset, count)])


def shards(record):
    bins = whitened_bins(record)
    own = lax.all_to_all(bins, "freq", split_axis=0, concat_axis=0, tiled=True)
    reach = lax.axis_size("chan") // 2
    return cross_all([own] + [upper_block(own, offset) for offset in range(1, reach + 1)])


def solution(mesh):
    return jax.shard_map(
        shards,
        mesh=mesh,
        in_specs=(P("freq", None, "chan"),),
        out_specs=P(None, "freq", "chan", None),
        check_vma=False,
    )
```

```python
import functools
import math

import jax
import jax.numpy as jnp
from jax import lax
from jax.experimental import pallas as pl
from jax.experimental.pallas import tpu as pltpu
from jax.sharding import PartitionSpec as P

NBIN = 64
NEIGH = 40
CHUNKS = 6
ROWS = 64
LANES = 128


def split_terms(x, rest=jnp.bfloat16):
    high = x.astype(jnp.bfloat16)
    return high, (x - high.astype(jnp.float32)).astype(rest)


def smoothed(power):
    row = lax.broadcasted_iota(jnp.int32, (NBIN, NBIN), 0)
    col = lax.broadcasted_iota(jnp.int32, (NBIN, NBIN), 1)
    below, above = NEIGH // 2, NEIGH - NEIGH // 2
    inside = ((col - row >= -below) & (col - row < above)).astype(jnp.float32)
    inside = inside.astype(jnp.bfloat16)
    high, rest = split_terms(power, jnp.float32)
    middle, low = split_terms(rest, jnp.bfloat16)
    total = jnp.dot(
        jnp.concatenate([inside, inside, inside], axis=1),
        jnp.concatenate([high, middle, low], axis=0),
        preferred_element_type=jnp.float32,
    )
    first = lax.broadcasted_iota(jnp.int32, power.shape, 0)
    count = jnp.minimum(first + above, NBIN) - jnp.maximum(first - below, 0)
    return total / count.astype(jnp.float32)


def base_angles(samples):
    stride, period = samples // (2 * NBIN), 2 * NBIN
    k = lax.broadcasted_iota(jnp.int32, (NBIN, period), 0)
    s = lax.broadcasted_iota(jnp.int32, (NBIN, period), 1)
    phase = s + stride * ((k * s) & (period - 1))
    return 2.0 * math.pi / samples * phase.astype(jnp.float32)


def whiten_kernel(samples, record_ref, out_ref, buf_ref, table_ref, sems):
    chunk = samples // CHUNKS
    period = 2 * NBIN
    turns = samples // period

    def fetch(n):
        part = pl.ds(n * chunk, chunk)
        return pltpu.make_async_copy(record_ref.at[0, part], buf_ref.at[part], sems.at[n])

    for n in range(CHUNKS):
        fetch(n).start()
    angle = base_angles(samples)
    cos, sin = jnp.cos(angle), jnp.sin(angle)
    for m in range(turns):
        c, s = math.cos(2.0 * math.pi * m / turns), math.sin(2.0 * math.pi * m / turns)
        part = pl.ds(m * period, period)
        table_ref[:NBIN, part] = (c * cos - s * sin).astype(jnp.bfloat16)
        table_ref[NBIN:, part] = (-(s * cos + c * sin)).astype(jnp.bfloat16)
    total = None
    for n in range(CHUNKS):
        fetch(n).wait()
        part = pl.ds(n * chunk, chunk)
        term = jnp.dot(table_ref[:, part], buf_ref[part], preferred_element_type=jnp.float32)
        total = term if total is None else total + term
    scaling = 1.0 / math.sqrt(samples)
    re, im = total[:NBIN] * scaling, total[NBIN:] * scaling
    power = 0.5 * (re * re + im * im)
    gain = lax.rsqrt(smoothed(power) + 1e-06)
    half = re.shape[1] // LANES
    for n in range(half):
        part = slice(n * LANES, (n + 1) * LANES)
        out_ref[:, n, :] = (re * gain)[:, part]
        out_ref[:, half + n, :] = (im * gain)[:, part]


def whitened_bins(record):
    _, samples, ch = record.shape
    return pl.pallas_call(
        functools.partial(whiten_kernel, samples),
        in_specs=[pl.BlockSpec(memory_space=pltpu.HBM)],
        out_specs=pl.BlockSpec(memory_space=pltpu.VMEM),
        out_shape=jax.ShapeDtypeStruct((NBIN, 2 * ch // LANES, LANES), jnp.float32),
        scratch_shapes=[
            pltpu.VMEM((samples, ch), jnp.bfloat16),
            pltpu.VMEM((2 * NBIN, samples), jnp.bfloat16),
            pltpu.SemaphoreType.DMA((CHUNKS,)),
        ],
        compiler_params=pltpu.CompilerParams(vmem_limit_bytes=52 * 1024 * 1024),
        name="whiten",
    )(record)


def real_imag(block_ref):
    half = block_ref.shape[1] // 2
    tiles = [block_ref[:, n, :] for n in range(2 * half)]
    return jnp.concatenate(tiles[:half], axis=1), jnp.concatenate(tiles[half:], axis=1)


def product(left_ref, block_ref, wide_ref, out_ref):
    re, im = real_imag(block_ref)
    high, low = split_terms(jnp.concatenate([re, im], axis=0))
    wide_ref[...] = jnp.concatenate([high, high, low], axis=0)
    halves, parts, rows, ch = out_ref.shape
    for a in range(halves):
        here = pl.ds(a * parts * rows, parts * rows)
        out_ref[a] = jnp.dot(
            left_ref[here], wide_ref[...], preferred_element_type=jnp.float32
        ).reshape(parts, rows, ch)


def own_kernel(own_ref, left_ref, prod_ref, wide_ref):
    re, im = real_imag(own_ref)
    scale = 1.0 / own_ref.shape[0]
    re, im = (re * scale).T, (im * scale).T
    rows = re.shape[0] // 2
    for a in range(2):
        r, i = re[a * rows:(a + 1) * rows], im[a * rows:(a + 1) * rows]
        left = jnp.concatenate(
            [jnp.concatenate([r, i], axis=1), jnp.concatenate([i, -r], axis=1)], axis=0
        )
        high, low = split_terms(left)
        left_ref[2 * a * rows:2 * (a + 1) * rows] = jnp.concatenate([high, low, high], axis=1)
    product(left_ref, own_ref, wide_ref, prod_ref)


def product_shape(ch):
    return jax.ShapeDtypeStruct((2, 2, ch // 2, ch), jnp.float32)


def own_terms(own):
    windows, pieces, lanes = own.shape
    ch = pieces * lanes // 2
    vmem = pl.BlockSpec(memory_space=pltpu.VMEM)
    return pl.pallas_call(
        own_kernel,
        in_specs=[vmem],
        out_specs=(vmem, vmem),
        out_shape=(
            jax.ShapeDtypeStruct((2 * ch, 6 * windows), jnp.bfloat16),
            product_shape(ch),
        ),
        scratch_shapes=[pltpu.VMEM((6 * windows, ch), jnp.bfloat16)],
        compiler_params=pltpu.CompilerParams(vmem_limit_bytes=16 * 1024 * 1024),
        cost_estimate=pl.CostEstimate(flops=0, bytes_accessed=1 << 20, transcendentals=0),
        name="own",
    )(own)


def region_kernel(first, given, keep, fresh, left_ref, *refs):
    count = len(given)
    blocks, refs = refs[:count], refs[count if fresh else count + 1:]
    out_ref, kept, refs = refs[0], refs[1:1 + len(keep)], refs[1 + len(keep):]
    wide_ref, prod_ref, band_ref, sems = refs
    products = []
    for n in range(count):
        if given[n]:
            products.append(blocks[n])
            continue
        target = kept[keep.index(n)] if n in keep else prod_ref.at[n]
        product(left_ref, blocks[n], wide_ref, target)
        products.append(target)
    ch = wide_ref.shape[1]
    rows = ch // 2
    tiles = ch // LANES
    row = lax.broadcasted_iota(jnp.int32, (ROWS, LANES), 0)
    lane = lax.broadcasted_iota(jnp.int32, (ROWS, LANES), 1)
    copies = []
    for a in range(2):
        for part in range(2):
            for start in range(0, rows, ROWS):
                source = (lane + row + start) % LANES
                stays = lane < LANES - start - row

                def turned(tile):
                    n, lanes = divmod(tile, tiles)
                    value = products[n][a, part, pl.ds(start, ROWS), pl.ds(lanes * LANES, LANES)]
                    return jnp.take_along_axis(value, source, axis=1, mode="promise_in_bounds")

                before = turned(a)
                for v in range((count - 1) * tiles):
                    after = turned(a + v + 1)
                    band_ref[part, pl.ds(a * rows + start, ROWS), pl.ds(v * LANES, LANES)] = (
                        jnp.where(stays, before, after)
                    )
                    before = after
            here = pl.ds(a * rows, rows)
            there = pl.ds(first * ch, (count - 1) * ch)
            copy = pltpu.make_async_copy(
                band_ref.at[part, here], out_ref.at[part, 0, here, there], sems.at[a, part]
            )
            copy.start()
            copies.append(copy)
    for copy in copies:
        copy.wait()


def region(left, blocks, first, band, out=None, keep=()):
    ch = left.shape[0] // 2
    depth = left.shape[1]
    count = len(blocks)
    vmem = pl.BlockSpec(memory_space=pltpu.VMEM)
    hbm = pl.BlockSpec(memory_space=pltpu.HBM)
    fresh = out is None
    given = tuple(block.ndim == 4 for block in blocks)
    return pl.pallas_call(
        functools.partial(region_kernel, first, given, keep, fresh),
        in_specs=[vmem] * (count + 1) + ([] if fresh else [hbm]),
        out_specs=(hbm,) + (vmem,) * len(keep),
        out_shape=(jax.ShapeDtypeStruct((2, 1, ch, band), jnp.float32),)
        + (product_shape(ch),) * len(keep),
        scratch_shapes=[
            pltpu.VMEM((depth, ch), jnp.bfloat16),
            pltpu.VMEM((count,) + product_shape(ch).shape, jnp.float32),
            pltpu.VMEM((2, ch, (count - 1) * ch), jnp.float32),
            pltpu.SemaphoreType.DMA((2, 2)),
        ],
        input_output_aliases={} if fresh else {count + 1: 0},
        compiler_params=pltpu.CompilerParams(vmem_limit_bytes=24 * 1024 * 1024),
        cost_estimate=pl.CostEstimate(flops=0, bytes_accessed=3 << 20, transcendentals=0),
        name="region",
    )(left, *blocks, *([] if fresh else [out]))


def cross_all(blocks):
    own, first, second, third, fourth = blocks
    _, pieces, lanes = own.shape
    band = (len(blocks) - 1) * pieces * lanes // 2
    left, own_product = own_terms(own)
    out, third_product = region(left, [third, fourth], 3, band, keep=(0,))
    out, second_product = region(left, [second, third_product], 2, band, out, keep=(0,))
    out, = region(left, [own_product, first, second_product], 0, band, out)
    return out


def upper_blocks(own):
    count = lax.axis_size("chan")
    half = count // 2

    def moved(array, pairs):
        return lax.ppermute(array, "chan", pairs)

    fourth, third, second = (
        moved(own, [(c, c - by) for c in range(by, count)]) for by in (half, 3, 2)
    )
    handed = jnp.where(lax.axis_index("chan") == 0, fourth, own)
    first = moved(
        handed, [(c, c - 1) for c in range(1, count) if c != half] + [(0, half - 1)]
    )
    return [first, second, third, fourth]


def shards(record):
    bins = whitened_bins(record)
    own = lax.all_to_all(bins, "freq", split_axis=0, concat_axis=0, tiled=True)
    return cross_all([own] + upper_blocks(own))


def solution(mesh):
    return jax.shard_map(
        shards,
        mesh=mesh,
        in_specs=(P("freq", None, "chan"),),
        out_specs=P(None, "freq", "chan", None),
        check_vma=False,
    )
```

```python
import functools
import math

import jax
import jax.numpy as jnp
from jax import lax
from jax.experimental import pallas as pl
from jax.experimental.pallas import tpu as pltpu
from jax.sharding import PartitionSpec as P

NBIN = 64
NEIGH = 40
CHUNKS = 6
ROWS = 64
LANES = 128


def split_terms(x, rest=jnp.bfloat16):
    high = x.astype(jnp.bfloat16)
    return high, (x - high.astype(jnp.float32)).astype(rest)


def smoothed(power):
    row = lax.broadcasted_iota(jnp.int32, (NBIN, NBIN), 0)
    col = lax.broadcasted_iota(jnp.int32, (NBIN, NBIN), 1)
    below, above = NEIGH // 2, NEIGH - NEIGH // 2
    inside = ((col - row >= -below) & (col - row < above)).astype(jnp.float32)
    inside = inside.astype(jnp.bfloat16)
    high, rest = split_terms(power, jnp.float32)
    middle, low = split_terms(rest, jnp.bfloat16)
    total = jnp.dot(
        jnp.concatenate([inside, inside, inside], axis=1),
        jnp.concatenate([high, middle, low], axis=0),
        preferred_element_type=jnp.float32,
    )
    first = lax.broadcasted_iota(jnp.int32, power.shape, 0)
    count = jnp.minimum(first + above, NBIN) - jnp.maximum(first - below, 0)
    return total / count.astype(jnp.float32)


def base_angles(samples):
    stride, period = samples // (2 * NBIN), 2 * NBIN
    k = lax.broadcasted_iota(jnp.int32, (NBIN, period), 0)
    s = lax.broadcasted_iota(jnp.int32, (NBIN, period), 1)
    phase = s + stride * ((k * s) & (period - 1))
    return 2.0 * math.pi / samples * phase.astype(jnp.float32)


def whiten_kernel(samples, record_ref, out_ref, buf_ref, table_ref, sems):
    chunk = samples // CHUNKS
    period = 2 * NBIN
    turns = samples // period

    def fetch(n):
        part = pl.ds(n * chunk, chunk)
        return pltpu.make_async_copy(record_ref.at[0, part], buf_ref.at[part], sems.at[n])

    for n in range(CHUNKS):
        fetch(n).start()
    angle = base_angles(samples)
    cos, sin = jnp.cos(angle), jnp.sin(angle)
    for m in range(turns):
        c, s = math.cos(2.0 * math.pi * m / turns), math.sin(2.0 * math.pi * m / turns)
        part = pl.ds(m * period, period)
        table_ref[:NBIN, part] = (c * cos - s * sin).astype(jnp.bfloat16)
        table_ref[NBIN:, part] = (-(s * cos + c * sin)).astype(jnp.bfloat16)
    total = None
    for n in range(CHUNKS):
        fetch(n).wait()
        part = pl.ds(n * chunk, chunk)
        term = jnp.dot(table_ref[:, part], buf_ref[part], preferred_element_type=jnp.float32)
        total = term if total is None else total + term
    scaling = 1.0 / math.sqrt(samples)
    re, im = total[:NBIN] * scaling, total[NBIN:] * scaling
    power = 0.5 * (re * re + im * im)
    gain = lax.rsqrt(smoothed(power) + 1e-06)
    half = re.shape[1] // LANES
    for n in range(half):
        part = slice(n * LANES, (n + 1) * LANES)
        out_ref[:, n, :] = (re * gain)[:, part]
        out_ref[:, half + n, :] = (im * gain)[:, part]


def whitened_bins(record):
    _, samples, ch = record.shape
    return pl.pallas_call(
        functools.partial(whiten_kernel, samples),
        in_specs=[pl.BlockSpec(memory_space=pltpu.HBM)],
        out_specs=pl.BlockSpec(memory_space=pltpu.VMEM),
        out_shape=jax.ShapeDtypeStruct((NBIN, 2 * ch // LANES, LANES), jnp.float32),
        scratch_shapes=[
            pltpu.VMEM((samples, ch), jnp.bfloat16),
            pltpu.VMEM((2 * NBIN, samples), jnp.bfloat16),
            pltpu.SemaphoreType.DMA((CHUNKS,)),
        ],
        compiler_params=pltpu.CompilerParams(vmem_limit_bytes=52 * 1024 * 1024),
        name="whiten",
    )(record)


def real_imag(block_ref):
    half = block_ref.shape[1] // 2
    tiles = [block_ref[:, n, :] for n in range(2 * half)]
    return jnp.concatenate(tiles[:half], axis=1), jnp.concatenate(tiles[half:], axis=1)


def spread(block_ref, wide_ref):
    re, im = real_imag(block_ref)
    high, low = split_terms(jnp.concatenate([re, im], axis=0))
    wide_ref[...] = jnp.concatenate([high, high, low], axis=0)


def product(left_ref, wide_ref, out_ref, half):
    _, parts, rows, ch = out_ref.shape
    here = pl.ds(half * parts * rows, parts * rows)
    out_ref[half] = jnp.dot(
        left_ref[here], wide_ref[...], preferred_element_type=jnp.float32
    ).reshape(parts, rows, ch)


def product_kernel(left_ref, block_ref, prod_ref, wide_ref):
    spread(block_ref, wide_ref)
    for half in range(2):
        product(left_ref, wide_ref, prod_ref, half)


def own_kernel(own_ref, left_ref, prod_ref, wide_ref):
    re, im = real_imag(own_ref)
    scale = 1.0 / own_ref.shape[0]
    re, im = (re * scale).T, (im * scale).T
    rows = re.shape[0] // 2
    for a in range(2):
        r, i = re[a * rows:(a + 1) * rows], im[a * rows:(a + 1) * rows]
        left = jnp.concatenate(
            [jnp.concatenate([r, i], axis=1), jnp.concatenate([i, -r], axis=1)], axis=0
        )
        high, low = split_terms(left)
        left_ref[2 * a * rows:2 * (a + 1) * rows] = jnp.concatenate([high, low, high], axis=1)
    product_kernel(left_ref, own_ref, prod_ref, wide_ref)


def product_shape(ch):
    return jax.ShapeDtypeStruct((2, 2, ch // 2, ch), jnp.float32)


def own_terms(own):
    windows, pieces, lanes = own.shape
    ch = pieces * lanes // 2
    vmem = pl.BlockSpec(memory_space=pltpu.VMEM)
    return pl.pallas_call(
        own_kernel,
        in_specs=[vmem],
        out_specs=(vmem, vmem),
        out_shape=(
            jax.ShapeDtypeStruct((2 * ch, 6 * windows), jnp.bfloat16),
            product_shape(ch),
        ),
        scratch_shapes=[pltpu.VMEM((6 * windows, ch), jnp.bfloat16)],
        compiler_params=pltpu.CompilerParams(vmem_limit_bytes=16 * 1024 * 1024),
        cost_estimate=pl.CostEstimate(flops=0, bytes_accessed=1 << 20, transcendentals=0),
        name="own",
    )(own)


def block_product(left, block):
    rows, depth = left.shape
    vmem = pl.BlockSpec(memory_space=pltpu.VMEM)
    return pl.pallas_call(
        product_kernel,
        in_specs=[vmem, vmem],
        out_specs=vmem,
        out_shape=product_shape(rows // 2),
        scratch_shapes=[pltpu.VMEM((depth, rows // 2), jnp.bfloat16)],
        compiler_params=pltpu.CompilerParams(vmem_limit_bytes=16 * 1024 * 1024),
        cost_estimate=pl.CostEstimate(flops=0, bytes_accessed=1 << 20, transcendentals=0),
        name="product",
    )(left, block)


def region_kernel(first, given, keep, fresh, left_ref, *refs):
    count = len(given)
    blocks, refs = refs[:count], refs[count if fresh else count + 1:]
    out_ref, kept, refs = refs[0], refs[1:1 + len(keep)], refs[1 + len(keep):]
    wide_ref, prod_ref, band_ref, sems = refs
    products = list(blocks)
    fresh_blocks = [n for n in range(count) if not given[n]]
    for n in fresh_blocks:
        spread(blocks[n], wide_ref.at[n])
        products[n] = kept[keep.index(n)] if n in keep else prod_ref.at[n]
    ch = wide_ref.shape[2]
    rows = ch // 2
    tiles = ch // LANES
    row = lax.broadcasted_iota(jnp.int32, (ROWS, LANES), 0)
    lane = lax.broadcasted_iota(jnp.int32, (ROWS, LANES), 1)
    copies = []
    for a in range(2):
        for n in fresh_blocks:
            product(left_ref, wide_ref.at[n], products[n], a)
        for part in range(2):
            for start in range(0, rows, ROWS):
                source = (lane + row + start) % LANES
                stays = lane < LANES - start - row

                def turned(tile):
                    n, lanes = divmod(tile, tiles)
                    value = products[n][a, part, pl.ds(start, ROWS), pl.ds(lanes * LANES, LANES)]
                    return jnp.take_along_axis(value, source, axis=1, mode="promise_in_bounds")

                before = turned(a)
                for v in range((count - 1) * tiles):
                    after = turned(a + v + 1)
                    band_ref[part, pl.ds(a * rows + start, ROWS), pl.ds(v * LANES, LANES)] = (
                        jnp.where(stays, before, after)
                    )
                    before = after
            here = pl.ds(a * rows, rows)
            there = pl.ds(first * ch, (count - 1) * ch)
            copy = pltpu.make_async_copy(
                band_ref.at[part, here], out_ref.at[part, 0, here, there], sems.at[a, part]
            )
            copy.start()
            copies.append(copy)
    for copy in copies:
        copy.wait()


def region(left, blocks, first, band, out=None, keep=()):
    ch = left.shape[0] // 2
    depth = left.shape[1]
    count = len(blocks)
    vmem = pl.BlockSpec(memory_space=pltpu.VMEM)
    hbm = pl.BlockSpec(memory_space=pltpu.HBM)
    fresh = out is None
    given = tuple(block.ndim == 4 for block in blocks)
    return pl.pallas_call(
        functools.partial(region_kernel, first, given, keep, fresh),
        in_specs=[vmem] * (count + 1) + ([] if fresh else [hbm]),
        out_specs=(hbm,) + (vmem,) * len(keep),
        out_shape=(jax.ShapeDtypeStruct((2, 1, ch, band), jnp.float32),)
        + (product_shape(ch),) * len(keep),
        scratch_shapes=[
            pltpu.VMEM((count, depth, ch), jnp.bfloat16),
            pltpu.VMEM((count,) + product_shape(ch).shape, jnp.float32),
            pltpu.VMEM((2, ch, (count - 1) * ch), jnp.float32),
            pltpu.SemaphoreType.DMA((2, 2)),
        ],
        input_output_aliases={} if fresh else {count + 1: 0},
        compiler_params=pltpu.CompilerParams(vmem_limit_bytes=24 * 1024 * 1024),
        cost_estimate=pl.CostEstimate(flops=0, bytes_accessed=3 << 20, transcendentals=0),
        name="region",
    )(left, *blocks, *([] if fresh else [out]))


def cross_all(blocks):
    own, first, second, third, fourth = blocks
    _, pieces, lanes = own.shape
    band = (len(blocks) - 1) * pieces * lanes // 2
    left, own_product = own_terms(own)
    fourth_product = block_product(left, fourth)
    out, first_product = region(left, [own_product, first], 0, band, keep=(1,))
    out, second_product = region(left, [first_product, second], 1, band, out, keep=(1,))
    out, = region(left, [second_product, third, fourth_product], 2, band, out)
    return out


def upper_blocks(own):
    count = lax.axis_size("chan")
    half = count // 2

    def moved(array, pairs):
        return lax.ppermute(array, "chan", pairs)

    fourth = moved(own, [(c, c - half) for c in range(half, count)])
    first = moved(own, [(c, c - 1) for c in range(1, count)])
    handed = jnp.where(lax.axis_index("chan") < 2, fourth, own)
    second = moved(
        handed,
        [(c, c - 2) for c in range(2, count) if c // half == (c - 2) // half]
        + [(c, c + 2) for c in range(2)],
    )
    third = moved(handed, [(c, c - 3) for c in range(3, count)])
    return [first, second, third, fourth]


def shards(record):
    bins = whitened_bins(record)
    own = lax.all_to_all(bins, "freq", split_axis=0, concat_axis=0, tiled=True)
    return cross_all([own] + upper_blocks(own))


def solution(mesh):
    return jax.shard_map(
        shards,
        mesh=mesh,
        in_specs=(P("freq", None, "chan"),),
        out_specs=P(None, "freq", "chan", None),
        check_vma=False,
    )
```

```python
import functools
import math

import jax
import jax.numpy as jnp
from jax import lax
from jax.experimental import pallas as pl
from jax.experimental.pallas import tpu as pltpu
from jax.sharding import PartitionSpec as P

NBIN = 64
NEIGH = 40
CHUNKS = 6
ROWS = 64
LANES = 128


def split_terms(x, rest=jnp.bfloat16):
    high = x.astype(jnp.bfloat16)
    return high, (x - high.astype(jnp.float32)).astype(rest)


def smoothed(power):
    row = lax.broadcasted_iota(jnp.int32, (NBIN, NBIN), 0)
    col = lax.broadcasted_iota(jnp.int32, (NBIN, NBIN), 1)
    below, above = NEIGH // 2, NEIGH - NEIGH // 2
    inside = ((col - row >= -below) & (col - row < above)).astype(jnp.float32)
    inside = inside.astype(jnp.bfloat16)
    high, rest = split_terms(power, jnp.float32)
    middle, low = split_terms(rest, jnp.bfloat16)
    total = jnp.dot(
        jnp.concatenate([inside, inside, inside], axis=1),
        jnp.concatenate([high, middle, low], axis=0),
        preferred_element_type=jnp.float32,
    )
    first = lax.broadcasted_iota(jnp.int32, power.shape, 0)
    count = jnp.minimum(first + above, NBIN) - jnp.maximum(first - below, 0)
    return total / count.astype(jnp.float32)


def base_angles(samples):
    stride, period = samples // (2 * NBIN), 2 * NBIN
    k = lax.broadcasted_iota(jnp.int32, (NBIN, period), 0)
    s = lax.broadcasted_iota(jnp.int32, (NBIN, period), 1)
    phase = s + stride * ((k * s) & (period - 1))
    return 2.0 * math.pi / samples * phase.astype(jnp.float32)


def whiten_kernel(samples, record_ref, out_ref, buf_ref, table_ref, sems):
    chunk = samples // CHUNKS
    period = 2 * NBIN
    turns = samples // period

    def fetch(n):
        part = pl.ds(n * chunk, chunk)
        return pltpu.make_async_copy(record_ref.at[0, part], buf_ref.at[part], sems.at[n])

    for n in range(CHUNKS):
        fetch(n).start()
    angle = base_angles(samples)
    cos, sin = jnp.cos(angle), jnp.sin(angle)
    for m in range(turns):
        c, s = math.cos(2.0 * math.pi * m / turns), math.sin(2.0 * math.pi * m / turns)
        part = pl.ds(m * period, period)
        table_ref[:NBIN, part] = (c * cos - s * sin).astype(jnp.bfloat16)
        table_ref[NBIN:, part] = (-(s * cos + c * sin)).astype(jnp.bfloat16)
    total = None
    for n in range(CHUNKS):
        fetch(n).wait()
        part = pl.ds(n * chunk, chunk)
        term = jnp.dot(table_ref[:, part], buf_ref[part], preferred_element_type=jnp.float32)
        total = term if total is None else total + term
    scaling = 1.0 / math.sqrt(samples)
    re, im = total[:NBIN] * scaling, total[NBIN:] * scaling
    power = 0.5 * (re * re + im * im)
    gain = lax.rsqrt(smoothed(power) + 1e-06)
    half = re.shape[1] // LANES
    for n in range(half):
        part = slice(n * LANES, (n + 1) * LANES)
        out_ref[:, n, :] = (re * gain)[:, part]
        out_ref[:, half + n, :] = (im * gain)[:, part]


def whitened_bins(record):
    _, samples, ch = record.shape
    return pl.pallas_call(
        functools.partial(whiten_kernel, samples),
        in_specs=[pl.BlockSpec(memory_space=pltpu.HBM)],
        out_specs=pl.BlockSpec(memory_space=pltpu.VMEM),
        out_shape=jax.ShapeDtypeStruct((NBIN, 2 * ch // LANES, LANES), jnp.float32),
        scratch_shapes=[
            pltpu.VMEM((samples, ch), jnp.bfloat16),
            pltpu.VMEM((2 * NBIN, samples), jnp.bfloat16),
            pltpu.SemaphoreType.DMA((CHUNKS,)),
        ],
        compiler_params=pltpu.CompilerParams(vmem_limit_bytes=52 * 1024 * 1024),
        name="whiten",
    )(record)


def real_imag(block_ref):
    half = block_ref.shape[1] // 2
    tiles = [block_ref[:, n, :] for n in range(2 * half)]
    return jnp.concatenate(tiles[:half], axis=1), jnp.concatenate(tiles[half:], axis=1)


def spread(block_ref, wide_ref):
    re, im = real_imag(block_ref)
    high, low = split_terms(jnp.concatenate([re, im], axis=0))
    wide_ref[...] = jnp.concatenate([high, high, low], axis=0)


def product(left_ref, wide_ref, out_ref, half):
    _, parts, rows, ch = out_ref.shape
    here = pl.ds(half * parts * rows, parts * rows)
    out_ref[half] = jnp.dot(
        left_ref[here], wide_ref[...], preferred_element_type=jnp.float32
    ).reshape(parts, rows, ch)


def product_kernel(left_ref, block_ref, prod_ref, wide_ref):
    spread(block_ref, wide_ref)
    for half in range(2):
        product(left_ref, wide_ref, prod_ref, half)


def own_kernel(own_ref, left_ref, prod_ref, wide_ref):
    re, im = real_imag(own_ref)
    scale = 1.0 / own_ref.shape[0]
    re, im = (re * scale).T, (im * scale).T
    rows = re.shape[0] // 2
    for a in range(2):
        r, i = re[a * rows:(a + 1) * rows], im[a * rows:(a + 1) * rows]
        left = jnp.concatenate(
            [jnp.concatenate([r, i], axis=1), jnp.concatenate([i, -r], axis=1)], axis=0
        )
        high, low = split_terms(left)
        left_ref[2 * a * rows:2 * (a + 1) * rows] = jnp.concatenate([high, low, high], axis=1)
    product_kernel(left_ref, own_ref, prod_ref, wide_ref)


def product_shape(ch):
    return jax.ShapeDtypeStruct((2, 2, ch // 2, ch), jnp.float32)


def own_terms(own):
    windows, pieces, lanes = own.shape
    ch = pieces * lanes // 2
    vmem = pl.BlockSpec(memory_space=pltpu.VMEM)
    return pl.pallas_call(
        own_kernel,
        in_specs=[vmem],
        out_specs=(vmem, vmem),
        out_shape=(
            jax.ShapeDtypeStruct((2 * ch, 6 * windows), jnp.bfloat16),
            product_shape(ch),
        ),
        scratch_shapes=[pltpu.VMEM((6 * windows, ch), jnp.bfloat16)],
        compiler_params=pltpu.CompilerParams(vmem_limit_bytes=16 * 1024 * 1024),
        cost_estimate=pl.CostEstimate(flops=0, bytes_accessed=1 << 20, transcendentals=0),
        name="own",
    )(own)


def block_product(left, block):
    rows, depth = left.shape
    vmem = pl.BlockSpec(memory_space=pltpu.VMEM)
    return pl.pallas_call(
        product_kernel,
        in_specs=[vmem, vmem],
        out_specs=vmem,
        out_shape=product_shape(rows // 2),
        scratch_shapes=[pltpu.VMEM((depth, rows // 2), jnp.bfloat16)],
        compiler_params=pltpu.CompilerParams(vmem_limit_bytes=16 * 1024 * 1024),
        cost_estimate=pl.CostEstimate(flops=0, bytes_accessed=1 << 20, transcendentals=0),
        name="product",
    )(left, block)


def region_kernel(first, given, keep, fresh, left_ref, *refs):
    count = len(given)
    blocks, refs = refs[:count], refs[count if fresh else count + 1:]
    out_ref, kept, refs = refs[0], refs[1:1 + len(keep)], refs[1 + len(keep):]
    wide_ref, prod_ref, band_ref, sems = refs
    products = list(blocks)
    fresh_blocks = [n for n in range(count) if not given[n]]
    for n in fresh_blocks:
        spread(blocks[n], wide_ref.at[n])
        products[n] = kept[keep.index(n)] if n in keep else prod_ref.at[n]
    ch = wide_ref.shape[2]
    rows = ch // 2
    tiles = ch // LANES
    row = lax.broadcasted_iota(jnp.int32, (ROWS, LANES), 0)
    lane = lax.broadcasted_iota(jnp.int32, (ROWS, LANES), 1)
    copies = []
    for a in range(2):
        for n in fresh_blocks:
            product(left_ref, wide_ref.at[n], products[n], a)
        for part in range(2):
            for start in range(0, rows, ROWS):
                source = (lane + row + start) % LANES
                stays = lane < LANES - start - row

                def turned(tile):
                    n, lanes = divmod(tile, tiles)
                    value = products[n][a, part, pl.ds(start, ROWS), pl.ds(lanes * LANES, LANES)]
                    return jnp.take_along_axis(value, source, axis=1, mode="promise_in_bounds")

                before = turned(a)
                for v in range((count - 1) * tiles):
                    after = turned(a + v + 1)
                    band_ref[part, pl.ds(a * rows + start, ROWS), pl.ds(v * LANES, LANES)] = (
                        jnp.where(stays, before, after)
                    )
                    before = after
            here = pl.ds(a * rows, rows)
            there = pl.ds(first * ch, (count - 1) * ch)
            copy = pltpu.make_async_copy(
                band_ref.at[part, here], out_ref.at[part, 0, here, there], sems.at[a, part]
            )
            copy.start()
            copies.append(copy)
    for copy in copies:
        copy.wait()


def region(left, blocks, first, band, out=None, keep=()):
    ch = left.shape[0] // 2
    depth = left.shape[1]
    count = len(blocks)
    vmem = pl.BlockSpec(memory_space=pltpu.VMEM)
    hbm = pl.BlockSpec(memory_space=pltpu.HBM)
    fresh = out is None
    given = tuple(block.ndim == 4 for block in blocks)
    return pl.pallas_call(
        functools.partial(region_kernel, first, given, keep, fresh),
        in_specs=[vmem] * (count + 1) + ([] if fresh else [hbm]),
        out_specs=(hbm,) + (vmem,) * len(keep),
        out_shape=(jax.ShapeDtypeStruct((2, 1, ch, band), jnp.float32),)
        + (product_shape(ch),) * len(keep),
        scratch_shapes=[
            pltpu.VMEM((count, depth, ch), jnp.bfloat16),
            pltpu.VMEM((count,) + product_shape(ch).shape, jnp.float32),
            pltpu.VMEM((2, ch, (count - 1) * ch), jnp.float32),
            pltpu.SemaphoreType.DMA((2, 2)),
        ],
        input_output_aliases={} if fresh else {count + 1: 0},
        compiler_params=pltpu.CompilerParams(vmem_limit_bytes=24 * 1024 * 1024),
        cost_estimate=pl.CostEstimate(flops=0, bytes_accessed=3 << 20, transcendentals=0),
        name="region",
    )(left, *blocks, *([] if fresh else [out]))


def cross_all(blocks):
    own, first, second, third, fourth = blocks
    _, pieces, lanes = own.shape
    band = (len(blocks) - 1) * pieces * lanes // 2
    left, own_product = own_terms(own)
    fourth_product = block_product(left, fourth)
    out, first_product = region(left, [own_product, first], 0, band, keep=(1,))
    out, second_product = region(left, [first_product, second], 1, band, out, keep=(1,))
    out, = region(left, [second_product, third, fourth_product], 2, band, out)
    return out


def upper_block(own, offset):
    count = lax.axis_size("chan")
    return lax.ppermute(own, "chan", [(c, c - offset) for c in range(offset, count)])


def shards(record):
    bins = whitened_bins(record)
    own = lax.all_to_all(bins, "freq", split_axis=0, concat_axis=0, tiled=True)
    reach = lax.axis_size("chan") // 2
    return cross_all([own] + [upper_block(own, offset) for offset in range(1, reach + 1)])


def solution(mesh):
    return jax.shard_map(
        shards,
        mesh=mesh,
        in_specs=(P("freq", None, "chan"),),
        out_specs=P(None, "freq", "chan", None),
        check_vma=False,
    )
```

```python
import functools
import math

import jax
import jax.numpy as jnp
from jax import lax
from jax.experimental import pallas as pl
from jax.experimental.pallas import tpu as pltpu
from jax.sharding import PartitionSpec as P

NBIN = 64
NEIGH = 40
CHUNKS = 6
ROWS = 8
LANES = 128


def split_terms(x, rest=jnp.bfloat16):
    high = x.astype(jnp.bfloat16)
    return high, (x - high.astype(jnp.float32)).astype(rest)


def smoothed(power):
    row = lax.broadcasted_iota(jnp.int32, (NBIN, NBIN), 0)
    col = lax.broadcasted_iota(jnp.int32, (NBIN, NBIN), 1)
    below, above = NEIGH // 2, NEIGH - NEIGH // 2
    inside = ((col - row >= -below) & (col - row < above)).astype(jnp.float32)
    inside = inside.astype(jnp.bfloat16)
    high, rest = split_terms(power, jnp.float32)
    middle, low = split_terms(rest, jnp.bfloat16)
    total = jnp.dot(
        jnp.concatenate([inside, inside, inside], axis=1),
        jnp.concatenate([high, middle, low], axis=0),
        preferred_element_type=jnp.float32,
    )
    first = lax.broadcasted_iota(jnp.int32, power.shape, 0)
    count = jnp.minimum(first + above, NBIN) - jnp.maximum(first - below, 0)
    return total / count.astype(jnp.float32)


def base_angles(samples):
    stride, period = samples // (2 * NBIN), 2 * NBIN
    k = lax.broadcasted_iota(jnp.int32, (NBIN, period), 0)
    s = lax.broadcasted_iota(jnp.int32, (NBIN, period), 1)
    phase = s + stride * ((k * s) & (period - 1))
    return 2.0 * math.pi / samples * phase.astype(jnp.float32)


def whiten_kernel(samples, record_ref, out_ref, buf_ref, table_ref, sems):
    chunk = samples // CHUNKS
    period = 2 * NBIN
    turns = samples // period

    def fetch(n):
        part = pl.ds(n * chunk, chunk)
        return pltpu.make_async_copy(record_ref.at[0, part], buf_ref.at[part], sems.at[n])

    for n in range(CHUNKS):
        fetch(n).start()
    angle = base_angles(samples)
    cos, sin = jnp.cos(angle), jnp.sin(angle)
    for m in range(turns):
        c, s = math.cos(2.0 * math.pi * m / turns), math.sin(2.0 * math.pi * m / turns)
        part = pl.ds(m * period, period)
        table_ref[:NBIN, part] = (c * cos - s * sin).astype(jnp.bfloat16)
        table_ref[NBIN:, part] = (-(s * cos + c * sin)).astype(jnp.bfloat16)
    total = None
    for n in range(CHUNKS):
        fetch(n).wait()
        part = pl.ds(n * chunk, chunk)
        term = jnp.dot(table_ref[:, part], buf_ref[part], preferred_element_type=jnp.float32)
        total = term if total is None else total + term
    scaling = 1.0 / math.sqrt(samples)
    re, im = total[:NBIN] * scaling, total[NBIN:] * scaling
    power = 0.5 * (re * re + im * im)
    gain = lax.rsqrt(smoothed(power) + 1e-06)
    half = re.shape[1] // LANES
    for n in range(half):
        part = slice(n * LANES, (n + 1) * LANES)
        out_ref[:, n, :] = (re * gain)[:, part]
        out_ref[:, half + n, :] = (im * gain)[:, part]


def whitened_bins(record):
    _, samples, ch = record.shape
    return pl.pallas_call(
        functools.partial(whiten_kernel, samples),
        in_specs=[pl.BlockSpec(memory_space=pltpu.HBM)],
        out_specs=pl.BlockSpec(memory_space=pltpu.VMEM),
        out_shape=jax.ShapeDtypeStruct((NBIN, 2 * ch // LANES, LANES), jnp.float32),
        scratch_shapes=[
            pltpu.VMEM((samples, ch), jnp.bfloat16),
            pltpu.VMEM((2 * NBIN, samples), jnp.bfloat16),
            pltpu.SemaphoreType.DMA((CHUNKS,)),
        ],
        compiler_params=pltpu.CompilerParams(vmem_limit_bytes=52 * 1024 * 1024),
        name="whiten",
    )(record)


def real_imag(block_ref):
    half = block_ref.shape[1] // 2
    tiles = [block_ref[:, n, :] for n in range(2 * half)]
    return jnp.concatenate(tiles[:half], axis=1), jnp.concatenate(tiles[half:], axis=1)


def spread(block_ref, wide_ref):
    re, im = real_imag(block_ref)
    high, low = split_terms(jnp.concatenate([re, im], axis=0))
    wide_ref[...] = jnp.concatenate([high, high, low], axis=0)


def product(left_ref, wide_ref, out_ref, half):
    _, parts, rows, ch = out_ref.shape
    here = pl.ds(half * parts * rows, parts * rows)
    out_ref[half] = jnp.dot(
        left_ref[here], wide_ref[...], preferred_element_type=jnp.float32
    ).reshape(parts, rows, ch)


def product_kernel(left_ref, block_ref, prod_ref, wide_ref):
    spread(block_ref, wide_ref)
    for half in range(2):
        product(left_ref, wide_ref, prod_ref, half)


def own_kernel(own_ref, left_ref, prod_ref, wide_ref):
    re, im = real_imag(own_ref)
    scale = 1.0 / own_ref.shape[0]
    re, im = (re * scale).T, (im * scale).T
    rows = re.shape[0] // 2
    for a in range(2):
        r, i = re[a * rows:(a + 1) * rows], im[a * rows:(a + 1) * rows]
        left = jnp.concatenate(
            [jnp.concatenate([r, i], axis=1), jnp.concatenate([i, -r], axis=1)], axis=0
        )
        high, low = split_terms(left)
        left_ref[2 * a * rows:2 * (a + 1) * rows] = jnp.concatenate([high, low, high], axis=1)
    product_kernel(left_ref, own_ref, prod_ref, wide_ref)


def product_shape(ch):
    return jax.ShapeDtypeStruct((2, 2, ch // 2, ch), jnp.float32)


def own_terms(own):
    windows, pieces, lanes = own.shape
    ch = pieces * lanes // 2
    vmem = pl.BlockSpec(memory_space=pltpu.VMEM)
    return pl.pallas_call(
        own_kernel,
        in_specs=[vmem],
        out_specs=(vmem, vmem),
        out_shape=(
            jax.ShapeDtypeStruct((2 * ch, 6 * windows), jnp.bfloat16),
            product_shape(ch),
        ),
        scratch_shapes=[pltpu.VMEM((6 * windows, ch), jnp.bfloat16)],
        compiler_params=pltpu.CompilerParams(vmem_limit_bytes=16 * 1024 * 1024),
        cost_estimate=pl.CostEstimate(flops=0, bytes_accessed=1 << 20, transcendentals=0),
        name="own",
    )(own)


def block_product(left, block):
    rows, depth = left.shape
    vmem = pl.BlockSpec(memory_space=pltpu.VMEM)
    return pl.pallas_call(
        product_kernel,
        in_specs=[vmem, vmem],
        out_specs=vmem,
        out_shape=product_shape(rows // 2),
        scratch_shapes=[pltpu.VMEM((depth, rows // 2), jnp.bfloat16)],
        compiler_params=pltpu.CompilerParams(vmem_limit_bytes=16 * 1024 * 1024),
        cost_estimate=pl.CostEstimate(flops=0, bytes_accessed=1 << 20, transcendentals=0),
        name="product",
    )(left, block)


def region_kernel(first, given, keep, fresh, left_ref, *refs):
    count = len(given)
    blocks, refs = refs[:count], refs[count if fresh else count + 1:]
    out_ref, kept, refs = refs[0], refs[1:1 + len(keep)], refs[1 + len(keep):]
    wide_ref, prod_ref, band_ref, sems = refs
    products = list(blocks)
    fresh_blocks = [n for n in range(count) if not given[n]]
    for n in fresh_blocks:
        spread(blocks[n], wide_ref.at[n])
        products[n] = kept[keep.index(n)] if n in keep else prod_ref.at[n]
    ch = wide_ref.shape[2]
    rows = ch // 2
    tiles = ch // LANES
    row = lax.broadcasted_iota(jnp.int32, (ROWS, LANES), 0)
    lane = lax.broadcasted_iota(jnp.int32, (ROWS, LANES), 1)
    copies = []
    for a in range(2):
        for n in fresh_blocks:
            product(left_ref, wide_ref.at[n], products[n], a)
        for start in range(0, rows, ROWS):
            source = (lane + row + start) % LANES
            stays = lane < LANES - start - row
            for part in range(2):

                def turned(tile):
                    n, lanes = divmod(tile, tiles)
                    value = products[n][a, part, pl.ds(start, ROWS), pl.ds(lanes * LANES, LANES)]
                    return jnp.take_along_axis(value, source, axis=1, mode="promise_in_bounds")

                before = turned(a)
                for v in range((count - 1) * tiles):
                    after = turned(a + v + 1)
                    band_ref[part, pl.ds(a * rows + start, ROWS), pl.ds(v * LANES, LANES)] = (
                        jnp.where(stays, before, after)
                    )
                    before = after
        for part in range(2):
            here = pl.ds(a * rows, rows)
            there = pl.ds(first * ch, (count - 1) * ch)
            copy = pltpu.make_async_copy(
                band_ref.at[part, here], out_ref.at[part, 0, here, there], sems.at[a, part]
            )
            copy.start()
            copies.append(copy)
    for copy in copies:
        copy.wait()


def region(left, blocks, first, band, out=None, keep=()):
    ch = left.shape[0] // 2
    depth = left.shape[1]
    count = len(blocks)
    vmem = pl.BlockSpec(memory_space=pltpu.VMEM)
    hbm = pl.BlockSpec(memory_space=pltpu.HBM)
    fresh = out is None
    given = tuple(block.ndim == 4 for block in blocks)
    return pl.pallas_call(
        functools.partial(region_kernel, first, given, keep, fresh),
        in_specs=[vmem] * (count + 1) + ([] if fresh else [hbm]),
        out_specs=(hbm,) + (vmem,) * len(keep),
        out_shape=(jax.ShapeDtypeStruct((2, 1, ch, band), jnp.float32),)
        + (product_shape(ch),) * len(keep),
        scratch_shapes=[
            pltpu.VMEM((count, depth, ch), jnp.bfloat16),
            pltpu.VMEM((count,) + product_shape(ch).shape, jnp.float32),
            pltpu.VMEM((2, ch, (count - 1) * ch), jnp.float32),
            pltpu.SemaphoreType.DMA((2, 2)),
        ],
        input_output_aliases={} if fresh else {count + 1: 0},
        compiler_params=pltpu.CompilerParams(vmem_limit_bytes=24 * 1024 * 1024),
        cost_estimate=pl.CostEstimate(flops=0, bytes_accessed=3 << 20, transcendentals=0),
        name="region",
    )(left, *blocks, *([] if fresh else [out]))


def cross_all(blocks):
    own, first, second, third, fourth = blocks
    _, pieces, lanes = own.shape
    band = (len(blocks) - 1) * pieces * lanes // 2
    left, own_product = own_terms(own)
    fourth_product = block_product(left, fourth)
    out, first_product = region(left, [own_product, first], 0, band, keep=(1,))
    second_product = block_product(left, second)
    out, = region(left, [first_product, second_product, third, fourth_product], 1, band, out)
    return out


def upper_block(own, offset):
    count = lax.axis_size("chan")
    return lax.ppermute(own, "chan", [(c, c - offset) for c in range(offset, count)])


def shards(record):
    bins = whitened_bins(record)
    own = lax.all_to_all(bins, "freq", split_axis=0, concat_axis=0, tiled=True)
    reach = lax.axis_size("chan") // 2
    return cross_all([own] + [upper_block(own, offset) for offset in range(1, reach + 1)])


def solution(mesh):
    return jax.shard_map(
        shards,
        mesh=mesh,
        in_specs=(P("freq", None, "chan"),),
        out_specs=P(None, "freq", "chan", None),
        check_vma=False,
    )
```

```python
import functools
import math

import jax
import jax.numpy as jnp
from jax import lax
from jax.experimental import pallas as pl
from jax.experimental.pallas import tpu as pltpu
from jax.sharding import Mesh, PartitionSpec as P

NBIN = 64
NEIGH = 40
GROUP = 8
CHUNKS = 6
ROWS = 8
LANES = 128


def split_terms(x, rest=jnp.bfloat16):
    high = x.astype(jnp.bfloat16)
    return high, (x - high.astype(jnp.float32)).astype(rest)


def bin_of(row):
    return (row & (GROUP - 1)) * GROUP + row // GROUP


def smoothed(power):
    row = bin_of(lax.broadcasted_iota(jnp.int32, (NBIN, NBIN), 0))
    col = bin_of(lax.broadcasted_iota(jnp.int32, (NBIN, NBIN), 1))
    below, above = NEIGH // 2, NEIGH - NEIGH // 2
    inside = ((col - row >= -below) & (col - row < above)).astype(jnp.float32)
    inside = inside.astype(jnp.bfloat16)
    high, rest = split_terms(power, jnp.float32)
    middle, low = split_terms(rest, jnp.bfloat16)
    total = jnp.dot(
        jnp.concatenate([inside, inside, inside], axis=1),
        jnp.concatenate([high, middle, low], axis=0),
        preferred_element_type=jnp.float32,
    )
    first = bin_of(lax.broadcasted_iota(jnp.int32, power.shape, 0))
    count = jnp.minimum(first + above, NBIN) - jnp.maximum(first - below, 0)
    return total / count.astype(jnp.float32)


def base_angles(samples):
    stride, period = samples // (2 * NBIN), 2 * NBIN
    k = bin_of(lax.broadcasted_iota(jnp.int32, (NBIN, period), 0))
    s = lax.broadcasted_iota(jnp.int32, (NBIN, period), 1)
    phase = s + stride * ((k * s) & (period - 1))
    return 2.0 * math.pi / samples * phase.astype(jnp.float32)


def whiten_kernel(samples, record_ref, out_ref, buf_ref, table_ref, sems):
    chunk = samples // CHUNKS
    period = 2 * NBIN
    turns = samples // period

    def fetch(n):
        part = pl.ds(n * chunk, chunk)
        return pltpu.make_async_copy(record_ref.at[0, part], buf_ref.at[part], sems.at[n])

    for n in range(CHUNKS):
        fetch(n).start()
    angle = base_angles(samples)
    cos, sin = jnp.cos(angle), jnp.sin(angle)
    for m in range(turns):
        c, s = math.cos(2.0 * math.pi * m / turns), math.sin(2.0 * math.pi * m / turns)
        part = pl.ds(m * period, period)
        table_ref[:NBIN, part] = (c * cos - s * sin).astype(jnp.bfloat16)
        table_ref[NBIN:, part] = (-(s * cos + c * sin)).astype(jnp.bfloat16)
    total = None
    for n in range(CHUNKS):
        fetch(n).wait()
        part = pl.ds(n * chunk, chunk)
        term = jnp.dot(table_ref[:, part], buf_ref[part], preferred_element_type=jnp.float32)
        total = term if total is None else total + term
    scaling = 1.0 / math.sqrt(samples)
    re, im = total[:NBIN] * scaling, total[NBIN:] * scaling
    power = 0.5 * (re * re + im * im)
    gain = lax.rsqrt(smoothed(power) + 1e-06)
    half = re.shape[1] // LANES
    for n in range(half):
        part = slice(n * LANES, (n + 1) * LANES)
        out_ref[:, n, :] = (re * gain)[:, part]
        out_ref[:, half + n, :] = (im * gain)[:, part]


def whitened_bins(record):
    _, samples, ch = record.shape
    return pl.pallas_call(
        functools.partial(whiten_kernel, samples),
        in_specs=[pl.BlockSpec(memory_space=pltpu.HBM)],
        out_specs=pl.BlockSpec(memory_space=pltpu.VMEM),
        out_shape=jax.ShapeDtypeStruct((NBIN, 2 * ch // LANES, LANES), jnp.float32),
        scratch_shapes=[
            pltpu.VMEM((samples, ch), jnp.bfloat16),
            pltpu.VMEM((2 * NBIN, samples), jnp.bfloat16),
            pltpu.SemaphoreType.DMA((CHUNKS,)),
        ],
        compiler_params=pltpu.CompilerParams(vmem_limit_bytes=52 * 1024 * 1024),
        name="whiten",
    )(record)


def real_imag(block_ref):
    half = block_ref.shape[1] // 2
    tiles = [block_ref[:, n, :] for n in range(2 * half)]
    return jnp.concatenate(tiles[:half], axis=1), jnp.concatenate(tiles[half:], axis=1)


def spread(block_ref, wide_ref):
    re, im = real_imag(block_ref)
    high, low = split_terms(jnp.concatenate([re, im], axis=0))
    wide_ref[...] = jnp.concatenate([high, high, low], axis=0)


def product(left_ref, wide_ref, out_ref, half):
    _, parts, rows, ch = out_ref.shape
    here = pl.ds(half * parts * rows, parts * rows)
    out_ref[half] = jnp.dot(
        left_ref[here], wide_ref[...], preferred_element_type=jnp.float32
    ).reshape(parts, rows, ch)


def product_kernel(left_ref, block_ref, *refs):
    prod_ref, wide_ref = refs[-2:]
    spread(block_ref, wide_ref)
    for half in range(2):
        product(left_ref, wide_ref, prod_ref, half)


def own_kernel(own_ref, left_ref, prod_ref, wide_ref):
    re, im = real_imag(own_ref)
    scale = 1.0 / own_ref.shape[0]
    re, im = (re * scale).T, (im * scale).T
    rows = re.shape[0] // 2
    for a in range(2):
        r, i = re[a * rows:(a + 1) * rows], im[a * rows:(a + 1) * rows]
        left = jnp.concatenate(
            [jnp.concatenate([r, i], axis=1), jnp.concatenate([i, -r], axis=1)], axis=0
        )
        high, low = split_terms(left)
        left_ref[2 * a * rows:2 * (a + 1) * rows] = jnp.concatenate([high, low, high], axis=1)
    product_kernel(left_ref, own_ref, prod_ref, wide_ref)


def product_shape(ch):
    return jax.ShapeDtypeStruct((2, 2, ch // 2, ch), jnp.float32)


def own_terms(own):
    windows, pieces, lanes = own.shape
    ch = pieces * lanes // 2
    vmem = pl.BlockSpec(memory_space=pltpu.VMEM)
    return pl.pallas_call(
        own_kernel,
        in_specs=[vmem],
        out_specs=(vmem, vmem),
        out_shape=(
            jax.ShapeDtypeStruct((2 * ch, 6 * windows), jnp.bfloat16),
            product_shape(ch),
        ),
        scratch_shapes=[pltpu.VMEM((6 * windows, ch), jnp.bfloat16)],
        compiler_params=pltpu.CompilerParams(vmem_limit_bytes=16 * 1024 * 1024),
        cost_estimate=pl.CostEstimate(flops=0, bytes_accessed=1 << 20, transcendentals=0),
        name="own",
    )(own)


def block_product(left, block, *after):
    rows, depth = left.shape
    vmem = pl.BlockSpec(memory_space=pltpu.VMEM)
    return pl.pallas_call(
        product_kernel,
        in_specs=[vmem, vmem] + [pl.BlockSpec(memory_space=pl.ANY)] * len(after),
        out_specs=vmem,
        out_shape=product_shape(rows // 2),
        scratch_shapes=[pltpu.VMEM((depth, rows // 2), jnp.bfloat16)],
        compiler_params=pltpu.CompilerParams(vmem_limit_bytes=16 * 1024 * 1024),
        cost_estimate=pl.CostEstimate(flops=0, bytes_accessed=1 << 20, transcendentals=0),
        name="product",
    )(left, block, *after)


def region_kernel(first, given, keep, fresh, left_ref, *refs):
    count = len(given)
    blocks, refs = refs[:count], refs[count if fresh else count + 1:]
    out_ref, kept, refs = refs[0], refs[1:1 + len(keep)], refs[1 + len(keep):]
    wide_ref, prod_ref, band_ref, sems = refs
    products = list(blocks)
    fresh_blocks = [n for n in range(count) if not given[n]]
    for n in fresh_blocks:
        spread(blocks[n], wide_ref.at[n])
        products[n] = kept[keep.index(n)] if n in keep else prod_ref.at[n]
    ch = wide_ref.shape[2]
    rows = ch // 2
    tiles = ch // LANES
    row = lax.broadcasted_iota(jnp.int32, (ROWS, LANES), 0)
    lane = lax.broadcasted_iota(jnp.int32, (ROWS, LANES), 1)
    copies = []
    for a in range(2):
        for n in fresh_blocks:
            product(left_ref, wide_ref.at[n], products[n], a)
        for start in range(0, rows, ROWS):
            source = (lane + row + start) % LANES
            stays = lane < LANES - start - row
            for part in range(2):

                def turned(tile):
                    n, lanes = divmod(tile, tiles)
                    value = products[n][a, part, pl.ds(start, ROWS), pl.ds(lanes * LANES, LANES)]
                    return jnp.take_along_axis(value, source, axis=1, mode="promise_in_bounds")

                before = turned(a)
                for v in range((count - 1) * tiles):
                    after = turned(a + v + 1)
                    band_ref[part, pl.ds(a * rows + start, ROWS), pl.ds(v * LANES, LANES)] = (
                        jnp.where(stays, before, after)
                    )
                    before = after
        for part in range(2):
            here = pl.ds(a * rows, rows)
            there = pl.ds(first * ch, (count - 1) * ch)
            copy = pltpu.make_async_copy(
                band_ref.at[part, here], out_ref.at[part, 0, here, there], sems.at[a, part]
            )
            copy.start()
            copies.append(copy)
    for copy in copies:
        copy.wait()


def region(left, blocks, first, band, out=None, keep=()):
    ch = left.shape[0] // 2
    depth = left.shape[1]
    count = len(blocks)
    vmem = pl.BlockSpec(memory_space=pltpu.VMEM)
    hbm = pl.BlockSpec(memory_space=pltpu.HBM)
    fresh = out is None
    given = tuple(block.ndim == 4 for block in blocks)
    return pl.pallas_call(
        functools.partial(region_kernel, first, given, keep, fresh),
        in_specs=[vmem] * (count + 1) + ([] if fresh else [hbm]),
        out_specs=(hbm,) + (vmem,) * len(keep),
        out_shape=(jax.ShapeDtypeStruct((2, 1, ch, band), jnp.float32),)
        + (product_shape(ch),) * len(keep),
        scratch_shapes=[
            pltpu.VMEM((count, depth, ch), jnp.bfloat16),
            pltpu.VMEM((count,) + product_shape(ch).shape, jnp.float32),
            pltpu.VMEM((2, ch, (count - 1) * ch), jnp.float32),
            pltpu.SemaphoreType.DMA((2, 2)),
        ],
        input_output_aliases={} if fresh else {count + 1: 0},
        compiler_params=pltpu.CompilerParams(vmem_limit_bytes=24 * 1024 * 1024),
        cost_estimate=pl.CostEstimate(flops=0, bytes_accessed=3 << 20, transcendentals=0),
        name="region",
    )(left, *blocks, *([] if fresh else [out]))


def cross_all(blocks):
    own, first, second, third, fourth = blocks
    _, pieces, lanes = own.shape
    band = (len(blocks) - 1) * pieces * lanes // 2
    left, own_product = own_terms(own)
    fourth_product = block_product(left, fourth)
    out, first_product = region(left, [own_product, first], 0, band, keep=(1,))
    second_product = block_product(left, second, first_product)
    out, = region(left, [first_product, second_product, third, fourth_product], 1, band, out)
    return out


def upper_block(own, offset):
    count = lax.axis_size("chan")
    return lax.ppermute(own, "chan", [(c, c - offset) for c in range(offset, count)])


def shards(record):
    bins = whitened_bins(record)
    own = lax.all_to_all(bins, ("g", "y"), split_axis=0, concat_axis=0, tiled=True)
    reach = lax.axis_size("chan") // 2
    return cross_all([own] + [upper_block(own, offset) for offset in range(1, reach + 1)])


def solution(mesh):
    fine = Mesh(mesh.devices.reshape(GROUP, GROUP, -1), ("y", "g", "chan"))
    return jax.shard_map(
        shards,
        mesh=fine,
        in_specs=(P(("y", "g"), None, "chan"),),
        out_specs=P(None, ("y", "g"), "chan", None),
        check_vma=False,
    )
```

```python
import functools
import math

import jax
import jax.numpy as jnp
from jax import lax
from jax.experimental import pallas as pl
from jax.experimental.pallas import tpu as pltpu
from jax.sharding import PartitionSpec as P

NBIN = 64
NEIGH = 40
CHUNKS = 6
ROWS = 8
LANES = 128


def split_terms(x, rest=jnp.bfloat16):
    high = x.astype(jnp.bfloat16)
    return high, (x - high.astype(jnp.float32)).astype(rest)


def bin_of(row):
    return (row & 7) * 8 + (3 - (row >> 4)) * 2 + ((row >> 3) & 1)


def smoothed(power):
    row = bin_of(lax.broadcasted_iota(jnp.int32, (NBIN, NBIN), 0))
    col = bin_of(lax.broadcasted_iota(jnp.int32, (NBIN, NBIN), 1))
    below, above = NEIGH // 2, NEIGH - NEIGH // 2
    inside = ((col - row >= -below) & (col - row < above)).astype(jnp.float32)
    inside = inside.astype(jnp.bfloat16)
    high, rest = split_terms(power, jnp.float32)
    middle, low = split_terms(rest, jnp.bfloat16)
    total = jnp.dot(
        jnp.concatenate([inside, inside, inside], axis=1),
        jnp.concatenate([high, middle, low], axis=0),
        preferred_element_type=jnp.float32,
    )
    first = bin_of(lax.broadcasted_iota(jnp.int32, power.shape, 0))
    count = jnp.minimum(first + above, NBIN) - jnp.maximum(first - below, 0)
    return total / count.astype(jnp.float32)


def base_angles(samples):
    stride, period = samples // (2 * NBIN), 2 * NBIN
    k = bin_of(lax.broadcasted_iota(jnp.int32, (NBIN, period), 0))
    s = lax.broadcasted_iota(jnp.int32, (NBIN, period), 1)
    phase = s + stride * ((k * s) & (period - 1))
    return 2.0 * math.pi / samples * phase.astype(jnp.float32)


def whiten_kernel(samples, record_ref, out_ref, buf_ref, table_ref, sems):
    chunk = samples // CHUNKS
    period = 2 * NBIN
    turns = samples // period

    def fetch(n):
        part = pl.ds(n * chunk, chunk)
        return pltpu.make_async_copy(record_ref.at[0, part], buf_ref.at[part], sems.at[n])

    for n in range(CHUNKS):
        fetch(n).start()
    angle = base_angles(samples)
    cos, sin = jnp.cos(angle), jnp.sin(angle)
    for m in range(turns):
        c, s = math.cos(2.0 * math.pi * m / turns), math.sin(2.0 * math.pi * m / turns)
        part = pl.ds(m * period, period)
        table_ref[:NBIN, part] = (c * cos - s * sin).astype(jnp.bfloat16)
        table_ref[NBIN:, part] = (-(s * cos + c * sin)).astype(jnp.bfloat16)
    total = None
    for n in range(CHUNKS):
        fetch(n).wait()
        part = pl.ds(n * chunk, chunk)
        term = jnp.dot(table_ref[:, part], buf_ref[part], preferred_element_type=jnp.float32)
        total = term if total is None else total + term
    scaling = 1.0 / math.sqrt(samples)
    re, im = total[:NBIN] * scaling, total[NBIN:] * scaling
    power = 0.5 * (re * re + im * im)
    gain = lax.rsqrt(smoothed(power) + 1e-06)
    half = re.shape[1] // LANES
    for n in range(half):
        part = slice(n * LANES, (n + 1) * LANES)
        out_ref[:, n, :] = (re * gain)[:, part]
        out_ref[:, half + n, :] = (im * gain)[:, part]


def whitened_bins(record):
    _, samples, ch = record.shape
    return pl.pallas_call(
        functools.partial(whiten_kernel, samples),
        in_specs=[pl.BlockSpec(memory_space=pltpu.HBM)],
        out_specs=pl.BlockSpec(memory_space=pltpu.VMEM),
        out_shape=jax.ShapeDtypeStruct((NBIN, 2 * ch // LANES, LANES), jnp.float32),
        scratch_shapes=[
            pltpu.VMEM((samples, ch), jnp.bfloat16),
            pltpu.VMEM((2 * NBIN, samples), jnp.bfloat16),
            pltpu.SemaphoreType.DMA((CHUNKS,)),
        ],
        compiler_params=pltpu.CompilerParams(vmem_limit_bytes=52 * 1024 * 1024),
        name="whiten",
    )(record)


def real_imag(block_ref):
    half = block_ref.shape[1] // 2
    tiles = [block_ref[:, n, :] for n in range(2 * half)]
    return jnp.concatenate(tiles[:half], axis=1), jnp.concatenate(tiles[half:], axis=1)


def spread(block_ref, wide_ref):
    re, im = real_imag(block_ref)
    high, low = split_terms(jnp.concatenate([re, im], axis=0))
    wide_ref[...] = jnp.concatenate([high, high, low], axis=0)


def product(left_ref, wide_ref, out_ref, half):
    _, parts, rows, ch = out_ref.shape
    here = pl.ds(half * parts * rows, parts * rows)
    out_ref[half] = jnp.dot(
        left_ref[here], wide_ref[...], preferred_element_type=jnp.float32
    ).reshape(parts, rows, ch)


def product_kernel(left_ref, block_ref, *refs):
    prod_ref, wide_ref = refs[-2:]
    spread(block_ref, wide_ref)
    for half in range(2):
        product(left_ref, wide_ref, prod_ref, half)


def own_kernel(own_ref, left_ref, prod_ref, wide_ref):
    re, im = real_imag(own_ref)
    scale = 1.0 / own_ref.shape[0]
    re, im = (re * scale).T, (im * scale).T
    rows = re.shape[0] // 2
    for a in range(2):
        r, i = re[a * rows:(a + 1) * rows], im[a * rows:(a + 1) * rows]
        left = jnp.concatenate(
            [jnp.concatenate([r, i], axis=1), jnp.concatenate([i, -r], axis=1)], axis=0
        )
        high, low = split_terms(left)
        left_ref[2 * a * rows:2 * (a + 1) * rows] = jnp.concatenate([high, low, high], axis=1)
    product_kernel(left_ref, own_ref, prod_ref, wide_ref)


def product_shape(ch):
    return jax.ShapeDtypeStruct((2, 2, ch // 2, ch), jnp.float32)


def own_terms(own):
    windows, pieces, lanes = own.shape
    ch = pieces * lanes // 2
    vmem = pl.BlockSpec(memory_space=pltpu.VMEM)
    return pl.pallas_call(
        own_kernel,
        in_specs=[vmem],
        out_specs=(vmem, vmem),
        out_shape=(
            jax.ShapeDtypeStruct((2 * ch, 6 * windows), jnp.bfloat16),
            product_shape(ch),
        ),
        scratch_shapes=[pltpu.VMEM((6 * windows, ch), jnp.bfloat16)],
        compiler_params=pltpu.CompilerParams(vmem_limit_bytes=16 * 1024 * 1024),
        cost_estimate=pl.CostEstimate(flops=0, bytes_accessed=1 << 20, transcendentals=0),
        name="own",
    )(own)


def block_product(left, block, *after):
    rows, depth = left.shape
    vmem = pl.BlockSpec(memory_space=pltpu.VMEM)
    return pl.pallas_call(
        product_kernel,
        in_specs=[vmem, vmem] + [pl.BlockSpec(memory_space=pl.ANY)] * len(after),
        out_specs=vmem,
        out_shape=product_shape(rows // 2),
        scratch_shapes=[pltpu.VMEM((depth, rows // 2), jnp.bfloat16)],
        compiler_params=pltpu.CompilerParams(vmem_limit_bytes=16 * 1024 * 1024),
        cost_estimate=pl.CostEstimate(flops=0, bytes_accessed=1 << 20, transcendentals=0),
        name="product",
    )(left, block, *after)


def region_kernel(first, given, keep, fresh, left_ref, *refs):
    count = len(given)
    blocks, refs = refs[:count], refs[count if fresh else count + 1:]
    out_ref, kept, refs = refs[0], refs[1:1 + len(keep)], refs[1 + len(keep):]
    wide_ref, prod_ref, band_ref, sems = refs
    products = list(blocks)
    fresh_blocks = [n for n in range(count) if not given[n]]
    for n in fresh_blocks:
        spread(blocks[n], wide_ref.at[n])
        products[n] = kept[keep.index(n)] if n in keep else prod_ref.at[n]
    ch = wide_ref.shape[2]
    rows = ch // 2
    tiles = ch // LANES
    row = lax.broadcasted_iota(jnp.int32, (ROWS, LANES), 0)
    lane = lax.broadcasted_iota(jnp.int32, (ROWS, LANES), 1)
    copies = []
    for a in range(2):
        for n in fresh_blocks:
            product(left_ref, wide_ref.at[n], products[n], a)
        for start in range(0, rows, ROWS):
            source = (lane + row + start) % LANES
            stays = lane < LANES - start - row
            for part in range(2):

                def turned(tile):
                    n, lanes = divmod(tile, tiles)
                    value = products[n][a, part, pl.ds(start, ROWS), pl.ds(lanes * LANES, LANES)]
                    return jnp.take_along_axis(value, source, axis=1, mode="promise_in_bounds")

                before = turned(a)
                for v in range((count - 1) * tiles):
                    after = turned(a + v + 1)
                    band_ref[part, pl.ds(a * rows + start, ROWS), pl.ds(v * LANES, LANES)] = (
                        jnp.where(stays, before, after)
                    )
                    before = after
        for part in range(2):
            here = pl.ds(a * rows, rows)
            there = pl.ds(first * ch, (count - 1) * ch)
            copy = pltpu.make_async_copy(
                band_ref.at[part, here], out_ref.at[part, 0, here, there], sems.at[a, part]
            )
            copy.start()
            copies.append(copy)
    for copy in copies:
        copy.wait()


def region(left, blocks, first, band, out=None, keep=()):
    ch = left.shape[0] // 2
    depth = left.shape[1]
    count = len(blocks)
    vmem = pl.BlockSpec(memory_space=pltpu.VMEM)
    hbm = pl.BlockSpec(memory_space=pltpu.HBM)
    fresh = out is None
    given = tuple(block.ndim == 4 for block in blocks)
    return pl.pallas_call(
        functools.partial(region_kernel, first, given, keep, fresh),
        in_specs=[vmem] * (count + 1) + ([] if fresh else [hbm]),
        out_specs=(hbm,) + (vmem,) * len(keep),
        out_shape=(jax.ShapeDtypeStruct((2, 1, ch, band), jnp.float32),)
        + (product_shape(ch),) * len(keep),
        scratch_shapes=[
            pltpu.VMEM((count, depth, ch), jnp.bfloat16),
            pltpu.VMEM((count,) + product_shape(ch).shape, jnp.float32),
            pltpu.VMEM((2, ch, (count - 1) * ch), jnp.float32),
            pltpu.SemaphoreType.DMA((2, 2)),
        ],
        input_output_aliases={} if fresh else {count + 1: 0},
        compiler_params=pltpu.CompilerParams(vmem_limit_bytes=24 * 1024 * 1024),
        cost_estimate=pl.CostEstimate(flops=0, bytes_accessed=3 << 20, transcendentals=0),
        name="region",
    )(left, *blocks, *([] if fresh else [out]))


def cross_all(blocks):
    own, first, second, third, fourth = blocks
    _, pieces, lanes = own.shape
    band = (len(blocks) - 1) * pieces * lanes // 2
    left, own_product = own_terms(own)
    fourth_product = block_product(left, fourth)
    out, first_product = region(left, [own_product, first], 0, band, keep=(1,))
    second_product = block_product(left, second, first_product)
    out, = region(left, [first_product, second_product, third, fourth_product], 1, band, out)
    return out


def upper_block(own, offset):
    count = lax.axis_size("chan")
    return lax.ppermute(own, "chan", [(c, c - offset) for c in range(offset, count)])


def shards(record):
    bins = whitened_bins(record)
    own = lax.all_to_all(
        bins, "freq", split_axis=0, concat_axis=0, tiled=True,
        axis_index_groups=[[bin_of(row) for row in range(NBIN)]],
    )
    reach = lax.axis_size("chan") // 2
    return cross_all([own] + [upper_block(own, offset) for offset in range(1, reach + 1)])


def solution(mesh):
    return jax.shard_map(
        shards,
        mesh=mesh,
        in_specs=(P("freq", None, "chan"),),
        out_specs=P(None, "freq", "chan", None),
        check_vma=False,
    )
```

```python
import functools
import math

import jax
import jax.numpy as jnp
from jax import lax
from jax.experimental import pallas as pl
from jax.experimental.pallas import tpu as pltpu
from jax.sharding import PartitionSpec as P

NBIN = 64
NEIGH = 40
CHUNKS = 6
ROWS = 8
LANES = 128


def split_terms(x, rest=jnp.bfloat16):
    high = x.astype(jnp.bfloat16)
    return high, (x - high.astype(jnp.float32)).astype(rest)


def bin_of(row):
    step = (row >> 1) & 3
    y = 4 + step - (row & 1) * (1 + 2 * step)
    return y * 8 + (3 - (row >> 4)) * 2 + ((row >> 3) & 1)


def smoothed(power):
    row = bin_of(lax.broadcasted_iota(jnp.int32, (NBIN, NBIN), 0))
    col = bin_of(lax.broadcasted_iota(jnp.int32, (NBIN, NBIN), 1))
    below, above = NEIGH // 2, NEIGH - NEIGH // 2
    inside = ((col - row >= -below) & (col - row < above)).astype(jnp.float32)
    inside = inside.astype(jnp.bfloat16)
    high, rest = split_terms(power, jnp.float32)
    middle, low = split_terms(rest, jnp.bfloat16)
    total = jnp.dot(
        jnp.concatenate([inside, inside, inside], axis=1),
        jnp.concatenate([high, middle, low], axis=0),
        preferred_element_type=jnp.float32,
    )
    first = bin_of(lax.broadcasted_iota(jnp.int32, power.shape, 0))
    count = jnp.minimum(first + above, NBIN) - jnp.maximum(first - below, 0)
    return total / count.astype(jnp.float32)


def base_angles(samples):
    stride, period = samples // (2 * NBIN), 2 * NBIN
    k = bin_of(lax.broadcasted_iota(jnp.int32, (NBIN, period), 0))
    s = lax.broadcasted_iota(jnp.int32, (NBIN, period), 1)
    phase = s + stride * ((k * s) & (period - 1))
    return 2.0 * math.pi / samples * phase.astype(jnp.float32)


def whiten_kernel(samples, record_ref, out_ref, buf_ref, table_ref, sems):
    chunk = samples // CHUNKS
    period = 2 * NBIN
    turns = samples // period

    def fetch(n):
        part = pl.ds(n * chunk, chunk)
        return pltpu.make_async_copy(record_ref.at[0, part], buf_ref.at[part], sems.at[n])

    for n in range(CHUNKS):
        fetch(n).start()
    angle = base_angles(samples)
    cos, sin = jnp.cos(angle), jnp.sin(angle)
    for m in range(turns):
        c, s = math.cos(2.0 * math.pi * m / turns), math.sin(2.0 * math.pi * m / turns)
        part = pl.ds(m * period, period)
        table_ref[:NBIN, part] = (c * cos - s * sin).astype(jnp.bfloat16)
        table_ref[NBIN:, part] = (-(s * cos + c * sin)).astype(jnp.bfloat16)
    total = None
    for n in range(CHUNKS):
        fetch(n).wait()
        part = pl.ds(n * chunk, chunk)
        term = jnp.dot(table_ref[:, part], buf_ref[part], preferred_element_type=jnp.float32)
        total = term if total is None else total + term
    scaling = 1.0 / math.sqrt(samples)
    re, im = total[:NBIN] * scaling, total[NBIN:] * scaling
    power = 0.5 * (re * re + im * im)
    gain = lax.rsqrt(smoothed(power) + 1e-06)
    half = re.shape[1] // LANES
    for n in range(half):
        part = slice(n * LANES, (n + 1) * LANES)
        out_ref[:, n, :] = (re * gain)[:, part]
        out_ref[:, half + n, :] = (im * gain)[:, part]


def whitened_bins(record):
    _, samples, ch = record.shape
    return pl.pallas_call(
        functools.partial(whiten_kernel, samples),
        in_specs=[pl.BlockSpec(memory_space=pltpu.HBM)],
        out_specs=pl.BlockSpec(memory_space=pltpu.VMEM),
        out_shape=jax.ShapeDtypeStruct((NBIN, 2 * ch // LANES, LANES), jnp.float32),
        scratch_shapes=[
            pltpu.VMEM((samples, ch), jnp.bfloat16),
            pltpu.VMEM((2 * NBIN, samples), jnp.bfloat16),
            pltpu.SemaphoreType.DMA((CHUNKS,)),
        ],
        compiler_params=pltpu.CompilerParams(vmem_limit_bytes=52 * 1024 * 1024),
        name="whiten",
    )(record)


def real_imag(block_ref):
    half = block_ref.shape[1] // 2
    tiles = [block_ref[:, n, :] for n in range(2 * half)]
    return jnp.concatenate(tiles[:half], axis=1), jnp.concatenate(tiles[half:], axis=1)


def spread(block_ref, wide_ref):
    re, im = real_imag(block_ref)
    high, low = split_terms(jnp.concatenate([re, im], axis=0))
    wide_ref[...] = jnp.concatenate([high, high, low], axis=0)


def product(left_ref, wide_ref, out_ref, half):
    _, parts, rows, ch = out_ref.shape
    here = pl.ds(half * parts * rows, parts * rows)
    out_ref[half] = jnp.dot(
        left_ref[here], wide_ref[...], preferred_element_type=jnp.float32
    ).reshape(parts, rows, ch)


def product_kernel(left_ref, block_ref, *refs):
    prod_ref, wide_ref = refs[-2:]
    spread(block_ref, wide_ref)
    for half in range(2):
        product(left_ref, wide_ref, prod_ref, half)


def own_kernel(own_ref, left_ref, prod_ref, wide_ref):
    re, im = real_imag(own_ref)
    scale = 1.0 / own_ref.shape[0]
    re, im = (re * scale).T, (im * scale).T
    rows = re.shape[0] // 2
    for a in range(2):
        r, i = re[a * rows:(a + 1) * rows], im[a * rows:(a + 1) * rows]
        left = jnp.concatenate(
            [jnp.concatenate([r, i], axis=1), jnp.concatenate([i, -r], axis=1)], axis=0
        )
        high, low = split_terms(left)
        left_ref[2 * a * rows:2 * (a + 1) * rows] = jnp.concatenate([high, low, high], axis=1)
    product_kernel(left_ref, own_ref, prod_ref, wide_ref)


def product_shape(ch):
    return jax.ShapeDtypeStruct((2, 2, ch // 2, ch), jnp.float32)


def own_terms(own):
    windows, pieces, lanes = own.shape
    ch = pieces * lanes // 2
    vmem = pl.BlockSpec(memory_space=pltpu.VMEM)
    return pl.pallas_call(
        own_kernel,
        in_specs=[vmem],
        out_specs=(vmem, vmem),
        out_shape=(
            jax.ShapeDtypeStruct((2 * ch, 6 * windows), jnp.bfloat16),
            product_shape(ch),
        ),
        scratch_shapes=[pltpu.VMEM((6 * windows, ch), jnp.bfloat16)],
        compiler_params=pltpu.CompilerParams(vmem_limit_bytes=16 * 1024 * 1024),
        cost_estimate=pl.CostEstimate(flops=0, bytes_accessed=1 << 20, transcendentals=0),
        name="own",
    )(own)


def block_product(left, block, *after):
    rows, depth = left.shape
    vmem = pl.BlockSpec(memory_space=pltpu.VMEM)
    return pl.pallas_call(
        product_kernel,
        in_specs=[vmem, vmem] + [pl.BlockSpec(memory_space=pl.ANY)] * len(after),
        out_specs=vmem,
        out_shape=product_shape(rows // 2),
        scratch_shapes=[pltpu.VMEM((depth, rows // 2), jnp.bfloat16)],
        compiler_params=pltpu.CompilerParams(vmem_limit_bytes=16 * 1024 * 1024),
        cost_estimate=pl.CostEstimate(flops=0, bytes_accessed=1 << 20, transcendentals=0),
        name="product",
    )(left, block, *after)


def region_kernel(first, given, keep, fresh, left_ref, *refs):
    count = len(given)
    blocks, refs = refs[:count], refs[count if fresh else count + 1:]
    out_ref, kept, refs = refs[0], refs[1:1 + len(keep)], refs[1 + len(keep):]
    wide_ref, prod_ref, band_ref, sems = refs
    products = list(blocks)
    fresh_blocks = [n for n in range(count) if not given[n]]
    for n in fresh_blocks:
        spread(blocks[n], wide_ref.at[n])
        products[n] = kept[keep.index(n)] if n in keep else prod_ref.at[n]
    ch = wide_ref.shape[2]
    rows = ch // 2
    tiles = ch // LANES
    row = lax.broadcasted_iota(jnp.int32, (ROWS, LANES), 0)
    lane = lax.broadcasted_iota(jnp.int32, (ROWS, LANES), 1)
    copies = []
    for a in range(2):
        for n in fresh_blocks:
            product(left_ref, wide_ref.at[n], products[n], a)
        for start in range(0, rows, ROWS):
            source = (lane + row + start) % LANES
            stays = lane < LANES - start - row
            for part in range(2):

                def turned(tile):
                    n, lanes = divmod(tile, tiles)
                    value = products[n][a, part, pl.ds(start, ROWS), pl.ds(lanes * LANES, LANES)]
                    return jnp.take_along_axis(value, source, axis=1, mode="promise_in_bounds")

                before = turned(a)
                for v in range((count - 1) * tiles):
                    after = turned(a + v + 1)
                    band_ref[part, pl.ds(a * rows + start, ROWS), pl.ds(v * LANES, LANES)] = (
                        jnp.where(stays, before, after)
                    )
                    before = after
        for part in range(2):
            here = pl.ds(a * rows, rows)
            there = pl.ds(first * ch, (count - 1) * ch)
            copy = pltpu.make_async_copy(
                band_ref.at[part, here], out_ref.at[part, 0, here, there], sems.at[a, part]
            )
            copy.start()
            copies.append(copy)
    for copy in copies:
        copy.wait()


def region(left, blocks, first, band, out=None, keep=()):
    ch = left.shape[0] // 2
    depth = left.shape[1]
    count = len(blocks)
    vmem = pl.BlockSpec(memory_space=pltpu.VMEM)
    hbm = pl.BlockSpec(memory_space=pltpu.HBM)
    fresh = out is None
    given = tuple(block.ndim == 4 for block in blocks)
    return pl.pallas_call(
        functools.partial(region_kernel, first, given, keep, fresh),
        in_specs=[vmem] * (count + 1) + ([] if fresh else [hbm]),
        out_specs=(hbm,) + (vmem,) * len(keep),
        out_shape=(jax.ShapeDtypeStruct((2, 1, ch, band), jnp.float32),)
        + (product_shape(ch),) * len(keep),
        scratch_shapes=[
            pltpu.VMEM((count, depth, ch), jnp.bfloat16),
            pltpu.VMEM((count,) + product_shape(ch).shape, jnp.float32),
            pltpu.VMEM((2, ch, (count - 1) * ch), jnp.float32),
            pltpu.SemaphoreType.DMA((2, 2)),
        ],
        input_output_aliases={} if fresh else {count + 1: 0},
        compiler_params=pltpu.CompilerParams(vmem_limit_bytes=24 * 1024 * 1024),
        cost_estimate=pl.CostEstimate(flops=0, bytes_accessed=3 << 20, transcendentals=0),
        name="region",
    )(left, *blocks, *([] if fresh else [out]))


def cross_all(blocks):
    own, first, second, third, fourth = blocks
    _, pieces, lanes = own.shape
    band = (len(blocks) - 1) * pieces * lanes // 2
    left, own_product = own_terms(own)
    fourth_product = block_product(left, fourth)
    out, first_product = region(left, [own_product, first], 0, band, keep=(1,))
    second_product = block_product(left, second, first_product)
    out, = region(left, [first_product, second_product, third, fourth_product], 1, band, out)
    return out


def upper_block(own, offset):
    count = lax.axis_size("chan")
    return lax.ppermute(own, "chan", [(c, c - offset) for c in range(offset, count)])


def shards(record):
    bins = whitened_bins(record)
    own = lax.all_to_all(
        bins, "freq", split_axis=0, concat_axis=0, tiled=True,
        axis_index_groups=[[bin_of(row) for row in range(NBIN)]],
    )
    reach = lax.axis_size("chan") // 2
    return cross_all([own] + [upper_block(own, offset) for offset in range(1, reach + 1)])


def solution(mesh):
    return jax.shard_map(
        shards,
        mesh=mesh,
        in_specs=(P("freq", None, "chan"),),
        out_specs=P(None, "freq", "chan", None),
        check_vma=False,
    )
```

```python
import functools
import math

import jax
import jax.numpy as jnp
from jax import lax
from jax.experimental import pallas as pl
from jax.experimental.pallas import tpu as pltpu
from jax.sharding import PartitionSpec as P

NBIN = 64
NEIGH = 40
CHUNKS = 6
ROWS = 8
LANES = 128


def split_terms(x, rest=jnp.bfloat16):
    high = x.astype(jnp.bfloat16)
    return high, (x - high.astype(jnp.float32)).astype(rest)


def bin_of(row):
    step = (row >> 2) & 3
    y = 4 + step - ((row >> 1) & 1) * (1 + 2 * step)
    return y * 8 + (3 - (row >> 4)) * 2 + (row & 1)


def smoothed(power):
    row = bin_of(lax.broadcasted_iota(jnp.int32, (NBIN, NBIN), 0))
    col = bin_of(lax.broadcasted_iota(jnp.int32, (NBIN, NBIN), 1))
    below, above = NEIGH // 2, NEIGH - NEIGH // 2
    inside = ((col - row >= -below) & (col - row < above)).astype(jnp.float32)
    inside = inside.astype(jnp.bfloat16)
    high, rest = split_terms(power, jnp.float32)
    middle, low = split_terms(rest, jnp.bfloat16)
    total = jnp.dot(
        jnp.concatenate([inside, inside, inside], axis=1),
        jnp.concatenate([high, middle, low], axis=0),
        preferred_element_type=jnp.float32,
    )
    first = bin_of(lax.broadcasted_iota(jnp.int32, power.shape, 0))
    count = jnp.minimum(first + above, NBIN) - jnp.maximum(first - below, 0)
    return total / count.astype(jnp.float32)


def base_angles(samples):
    stride, period = samples // (2 * NBIN), 2 * NBIN
    k = bin_of(lax.broadcasted_iota(jnp.int32, (NBIN, period), 0))
    s = lax.broadcasted_iota(jnp.int32, (NBIN, period), 1)
    phase = s + stride * ((k * s) & (period - 1))
    return 2.0 * math.pi / samples * phase.astype(jnp.float32)


def whiten_kernel(samples, record_ref, out_ref, buf_ref, table_ref, sems):
    chunk = samples // CHUNKS
    period = 2 * NBIN
    turns = samples // period

    def fetch(n):
        part = pl.ds(n * chunk, chunk)
        return pltpu.make_async_copy(record_ref.at[0, part], buf_ref.at[part], sems.at[n])

    for n in range(CHUNKS):
        fetch(n).start()
    angle = base_angles(samples)
    cos, sin = jnp.cos(angle), jnp.sin(angle)
    for m in range(turns):
        c, s = math.cos(2.0 * math.pi * m / turns), math.sin(2.0 * math.pi * m / turns)
        part = pl.ds(m * period, period)
        table_ref[:NBIN, part] = (c * cos - s * sin).astype(jnp.bfloat16)
        table_ref[NBIN:, part] = (-(s * cos + c * sin)).astype(jnp.bfloat16)
    total = None
    for n in range(CHUNKS):
        fetch(n).wait()
        part = pl.ds(n * chunk, chunk)
        term = jnp.dot(table_ref[:, part], buf_ref[part], preferred_element_type=jnp.float32)
        total = term if total is None else total + term
    scaling = 1.0 / math.sqrt(samples)
    re, im = total[:NBIN] * scaling, total[NBIN:] * scaling
    power = 0.5 * (re * re + im * im)
    gain = lax.rsqrt(smoothed(power) + 1e-06)
    half = re.shape[1] // LANES
    for n in range(half):
        part = slice(n * LANES, (n + 1) * LANES)
        out_ref[:, n, :] = (re * gain)[:, part]
        out_ref[:, half + n, :] = (im * gain)[:, part]


def whitened_bins(record):
    _, samples, ch = record.shape
    return pl.pallas_call(
        functools.partial(whiten_kernel, samples),
        in_specs=[pl.BlockSpec(memory_space=pltpu.HBM)],
        out_specs=pl.BlockSpec(memory_space=pltpu.VMEM),
        out_shape=jax.ShapeDtypeStruct((NBIN, 2 * ch // LANES, LANES), jnp.float32),
        scratch_shapes=[
            pltpu.VMEM((samples, ch), jnp.bfloat16),
            pltpu.VMEM((2 * NBIN, samples), jnp.bfloat16),
            pltpu.SemaphoreType.DMA((CHUNKS,)),
        ],
        compiler_params=pltpu.CompilerParams(vmem_limit_bytes=52 * 1024 * 1024),
        name="whiten",
    )(record)


def real_imag(block_ref):
    half = block_ref.shape[1] // 2
    tiles = [block_ref[:, n, :] for n in range(2 * half)]
    return jnp.concatenate(tiles[:half], axis=1), jnp.concatenate(tiles[half:], axis=1)


def spread(block_ref, wide_ref):
    re, im = real_imag(block_ref)
    high, low = split_terms(jnp.concatenate([re, im], axis=0))
    wide_ref[...] = jnp.concatenate([high, high, low], axis=0)


def product(left_ref, wide_ref, out_ref, half):
    _, parts, rows, ch = out_ref.shape
    here = pl.ds(half * parts * rows, parts * rows)
    out_ref[half] = jnp.dot(
        left_ref[here], wide_ref[...], preferred_element_type=jnp.float32
    ).reshape(parts, rows, ch)


def product_kernel(left_ref, block_ref, *refs):
    prod_ref, wide_ref = refs[-2:]
    spread(block_ref, wide_ref)
    for half in range(2):
        product(left_ref, wide_ref, prod_ref, half)


def own_kernel(own_ref, left_ref, prod_ref, wide_ref):
    re, im = real_imag(own_ref)
    scale = 1.0 / own_ref.shape[0]
    re, im = (re * scale).T, (im * scale).T
    rows = re.shape[0] // 2
    for a in range(2):
        r, i = re[a * rows:(a + 1) * rows], im[a * rows:(a + 1) * rows]
        left = jnp.concatenate(
            [jnp.concatenate([r, i], axis=1), jnp.concatenate([i, -r], axis=1)], axis=0
        )
        high, low = split_terms(left)
        left_ref[2 * a * rows:2 * (a + 1) * rows] = jnp.concatenate([high, low, high], axis=1)
    product_kernel(left_ref, own_ref, prod_ref, wide_ref)


def product_shape(ch):
    return jax.ShapeDtypeStruct((2, 2, ch // 2, ch), jnp.float32)


def own_terms(own):
    windows, pieces, lanes = own.shape
    ch = pieces * lanes // 2
    vmem = pl.BlockSpec(memory_space=pltpu.VMEM)
    return pl.pallas_call(
        own_kernel,
        in_specs=[vmem],
        out_specs=(vmem, vmem),
        out_shape=(
            jax.ShapeDtypeStruct((2 * ch, 6 * windows), jnp.bfloat16),
            product_shape(ch),
        ),
        scratch_shapes=[pltpu.VMEM((6 * windows, ch), jnp.bfloat16)],
        compiler_params=pltpu.CompilerParams(vmem_limit_bytes=16 * 1024 * 1024),
        cost_estimate=pl.CostEstimate(flops=0, bytes_accessed=1 << 20, transcendentals=0),
        name="own",
    )(own)


def block_product(left, block, *after):
    rows, depth = left.shape
    vmem = pl.BlockSpec(memory_space=pltpu.VMEM)
    return pl.pallas_call(
        product_kernel,
        in_specs=[vmem, vmem] + [pl.BlockSpec(memory_space=pl.ANY)] * len(after),
        out_specs=vmem,
        out_shape=product_shape(rows // 2),
        scratch_shapes=[pltpu.VMEM((depth, rows // 2), jnp.bfloat16)],
        compiler_params=pltpu.CompilerParams(vmem_limit_bytes=16 * 1024 * 1024),
        cost_estimate=pl.CostEstimate(flops=0, bytes_accessed=1 << 20, transcendentals=0),
        name="product",
    )(left, block, *after)


def region_kernel(first, given, keep, fresh, left_ref, *refs):
    count = len(given)
    blocks, refs = refs[:count], refs[count if fresh else count + 1:]
    out_ref, kept, refs = refs[0], refs[1:1 + len(keep)], refs[1 + len(keep):]
    wide_ref, prod_ref, band_ref, sems = refs
    products = list(blocks)
    fresh_blocks = [n for n in range(count) if not given[n]]
    for n in fresh_blocks:
        spread(blocks[n], wide_ref.at[n])
        products[n] = kept[keep.index(n)] if n in keep else prod_ref.at[n]
    ch = wide_ref.shape[2]
    rows = ch // 2
    tiles = ch // LANES
    row = lax.broadcasted_iota(jnp.int32, (ROWS, LANES), 0)
    lane = lax.broadcasted_iota(jnp.int32, (ROWS, LANES), 1)
    copies = []
    for a in range(2):
        for n in fresh_blocks:
            product(left_ref, wide_ref.at[n], products[n], a)
        for start in range(0, rows, ROWS):
            source = (lane + row + start) % LANES
            stays = lane < LANES - start - row
            for part in range(2):

                def turned(tile):
                    n, lanes = divmod(tile, tiles)
                    value = products[n][a, part, pl.ds(start, ROWS), pl.ds(lanes * LANES, LANES)]
                    return jnp.take_along_axis(value, source, axis=1, mode="promise_in_bounds")

                before = turned(a)
                for v in range((count - 1) * tiles):
                    after = turned(a + v + 1)
                    band_ref[part, pl.ds(a * rows + start, ROWS), pl.ds(v * LANES, LANES)] = (
                        jnp.where(stays, before, after)
                    )
                    before = after
        for part in range(2):
            here = pl.ds(a * rows, rows)
            there = pl.ds(first * ch, (count - 1) * ch)
            copy = pltpu.make_async_copy(
                band_ref.at[part, here], out_ref.at[part, 0, here, there], sems.at[a, part]
            )
            copy.start()
            copies.append(copy)
    for copy in copies:
        copy.wait()


def region(left, blocks, first, band, out=None, keep=()):
    ch = left.shape[0] // 2
    depth = left.shape[1]
    count = len(blocks)
    vmem = pl.BlockSpec(memory_space=pltpu.VMEM)
    hbm = pl.BlockSpec(memory_space=pltpu.HBM)
    fresh = out is None
    given = tuple(block.ndim == 4 for block in blocks)
    return pl.pallas_call(
        functools.partial(region_kernel, first, given, keep, fresh),
        in_specs=[vmem] * (count + 1) + ([] if fresh else [hbm]),
        out_specs=(hbm,) + (vmem,) * len(keep),
        out_shape=(jax.ShapeDtypeStruct((2, 1, ch, band), jnp.float32),)
        + (product_shape(ch),) * len(keep),
        scratch_shapes=[
            pltpu.VMEM((count, depth, ch), jnp.bfloat16),
            pltpu.VMEM((count,) + product_shape(ch).shape, jnp.float32),
            pltpu.VMEM((2, ch, (count - 1) * ch), jnp.float32),
            pltpu.SemaphoreType.DMA((2, 2)),
        ],
        input_output_aliases={} if fresh else {count + 1: 0},
        compiler_params=pltpu.CompilerParams(vmem_limit_bytes=24 * 1024 * 1024),
        cost_estimate=pl.CostEstimate(flops=0, bytes_accessed=3 << 20, transcendentals=0),
        name="region",
    )(left, *blocks, *([] if fresh else [out]))


def cross_all(blocks):
    own, first, second, third, fourth = blocks
    _, pieces, lanes = own.shape
    band = (len(blocks) - 1) * pieces * lanes // 2
    left, own_product = own_terms(own)
    fourth_product = block_product(left, fourth)
    out, first_product = region(left, [own_product, first], 0, band, keep=(1,))
    second_product = block_product(left, second, first_product)
    out, = region(left, [first_product, second_product, third, fourth_product], 1, band, out)
    return out


def upper_block(own, offset):
    count = lax.axis_size("chan")
    return lax.ppermute(own, "chan", [(c, c - offset) for c in range(offset, count)])


def shards(record):
    bins = whitened_bins(record)
    own = lax.all_to_all(
        bins, "freq", split_axis=0, concat_axis=0, tiled=True,
        axis_index_groups=[[bin_of(row) for row in range(NBIN)]],
    )
    reach = lax.axis_size("chan") // 2
    return cross_all([own] + [upper_block(own, offset) for offset in range(1, reach + 1)])


def solution(mesh):
    return jax.shard_map(
        shards,
        mesh=mesh,
        in_specs=(P("freq", None, "chan"),),
        out_specs=P(None, "freq", "chan", None),
        check_vma=False,
    )
```
